256 devices in a mesh: dp: 32 (over z, y), tensor: 8 (over x, core).
Axes of the slice: x: 4, y: 4, z: 8, core: 2. Of those that a mesh axis runs over, the one named last changes fastest.
Arguments:
- queries: bfloat16 [16384, 4096], P('dp', 'tensor'), may hold values from -20 to 20
- cotangent: bfloat16 [16384, 4096], P('dp', 'tensor'), may hold values from -6 to 6
- table: bfloat16 [512, 128, 896], P('dp'), may hold values from -6 to 6
- key_weight: bfloat16 [896, 4096], P(None, 'tensor'), may hold values from -0.1875 to 0.1875
- value_weight: bfloat16 [896, 4096], P(None, 'tensor'), may hold values from -0.1875 to 0.1875
- owners: int32 [256, 2], P('dp'), may hold values from 0 to 31, all different within a row; in each aligned block of 8 rows (0 to 7, 8 to 15, ...) at most 2 rows name the same one
- slots: int32 [256, 2], P('dp'), may hold values from 0 to 15
Outputs:
- attended: bfloat16 [16384, 4096], P('dp', 'tensor')
- d_query: bfloat16 [16384, 4096], P('dp', 'tensor')
- d_table: float32 [512, 128, 896], P('dp', 'tensor')
The draws below stay inside these ranges and needn't reach their ends.
Inputs may be any that keep to these rules, and one draw needn't show every extreme that they name: `owners`: in each aligned block of 8 rows (the spans of one dp index) no value occurs more than 2 times, and in some block one value occurs exactly 2 times; the two entries of a row differ.
All inputs are finite; a program needn't handle non-finite values.
Results may differ from the reference program's by a relative error of at most 0.0055.
The reference program's roundings to bfloat16 on the way (of `neighbours`, `keys`, `weights`, `dscores` and `d_keys`) count: a program that leaves them out, or rounds other values in their place, can miss the bound.
Values may be sent and summed in bfloat16 or wider, within the bound.
A program may use at most 128 MiB of HBM per device.

```python
import math
import jax
import jax.numpy as jnp
import numpy as np
from jax import lax

ENC = 896
HEADS = 32
HD = 128
SPAN = 64
NLEN = 128
CH_DEV = 8
SLABS_DEV = 16
CAP = 2
SPANS = 256
TOKENS = 16384
SLABS = 512
N_DP = 32


def draw_queries(key, part):
    key = jax.random.fold_in(key, 11)
    first_key = jax.random.fold_in(key, 0)
    entries = jnp.clip(jax.random.normal(first_key, (TOKENS, HEADS * HD), jnp.float32), -5.0, 5.0)
    return entries.astype(jnp.bfloat16)


def plant(values, own_key, smallest, largest):
    dims = values.shape
    spot = [jax.random.randint(jax.random.fold_in(own_key, axis), (), 0, dims[axis]) for axis in range(len(dims))]
    values = values.at[tuple(spot)].set(smallest)
    longest = dims.index(max(dims))
    spot[longest] = (spot[longest] + 1) % dims[longest]
    return values.at[tuple(spot)].set(largest)


def block_levels(stream_key, shape, cuts, smallest, largest):
    loudness, own = 1.0, jax.random.fold_in(stream_key, 6)
    for position, parts in cuts:
        steps = jnp.exp(jax.random.uniform(jax.random.fold_in(own, position), (parts,), jnp.float32, smallest / len(cuts), largest / len(cuts)))
        loudness = loudness * jnp.repeat(steps, shape[position] // parts).reshape([-1 if axis == position else 1 for axis in range(len(shape))])
    return loudness


def assign_block(rng, own, number, rows, count, top, bound, skew):
    order = jax.random.permutation(rng, count)
    heavy_load, usual = load_shares(count, rows * top, bound, skew, True), load_shares(count, rows * top, bound, skew, False)
    places = jnp.arange(count)

    def named(tallies, turn):
        used = int((tallies > 0).sum())
        fixed = max(1, used // 4)
        passed = fixed + (places - fixed + turn * (used - fixed)) % max(1, count - fixed)
        return jnp.zeros((count,), jnp.int32).at[order[jnp.where(places < fixed, places, passed)]].set(jnp.asarray(tallies, jnp.int32))

    tallies = jnp.where(number % 4 == 0, named(heavy_load, number // 4), named(usual, number - number // 4 - 1))
    mixed = jax.random.permutation(jax.random.fold_in(own, 3), count)
    giver, taker = mixed[0:count // 2 * 2:2], mixed[1:count // 2 * 2:2]
    room = jnp.minimum(tallies[giver] - 1, bound - tallies[taker]) // 2
    room = jnp.where((giver == order[0]) | (taker == order[0]) | (tallies[taker] == 0), 0, jnp.maximum(room, 0))
    passed = jax.random.randint(jax.random.fold_in(own, 4), (count // 2,), 0, 1 << 20) % (room + 1)
    tallies = tallies.at[giver].add(-passed).at[taker].add(passed)
    members = jnp.searchsorted(jnp.cumsum(tallies), jnp.arange(rows * top), side="right").astype(jnp.int32)
    table = members.reshape(top, rows).T
    table = table[jax.random.permutation(jax.random.fold_in(own, 1), rows)]
    turn = jax.random.randint(jax.random.fold_in(own, 2), (rows, 1), 0, top)
    return jnp.take_along_axis(table, (jnp.arange(top)[None, :] + turn) % top, axis=1)


def load_shares(count, total, limit, skew, full):
    portions = [(1 << 20) // math.isqrt(standing ** skew) + 1 for standing in range(1, count + 1)]
    largest = limit if full else min(limit, max(-(-total // count), total * portions[0] // sum(portions)))
    least = 1 if total - largest >= count - 1 else 0
    counts, spare = [largest] + [least] * (count - 1), total - largest - least * (count - 1)
    while spare > 0:
        free = [i for i in range(1, count) if counts[i] < largest] or [i for i in range(1, count) if counts[i] < limit]
        whole, budget = sum([portions[i] for i in free]), spare
        for i in free:
            extra = min(limit - counts[i], max(1, budget * portions[i] // whole), spare)
            counts[i] = counts[i] + extra
            spare = spare - extra
    return np.array(counts)


def bell_draw(stream_key, extent, scale, reach, pieces=(), kind=jnp.bfloat16):
    gain = block_levels(stream_key, extent, pieces, -0.22, 0.18) if pieces else 1.0
    values = jax.random.normal(stream_key, extent, jnp.float32) * scale * gain
    return jnp.minimum(jnp.maximum(values, -reach), reach).astype(kind)


def setup_inputs(seed: int = 0) -> dict:
    splits = jax.random.split(jax.random.key(seed), 8)
    queries = draw_queries(jax.random.fold_in(splits[7], 71), 0)
    cotangent = bell_draw(splits[1], (TOKENS, HEADS * HD), 1.0, 6.0, ((0, 32), (1, 8)))
    table = bell_draw(splits[2], (SLABS, NLEN, ENC), 1.0, 6.0, ((0, 32),))
    key_weight = bell_draw(splits[3], (ENC, HEADS * HD), ENC ** -0.5, 0.1875, ((1, 8),))
    value_weight = bell_draw(splits[4], (ENC, HEADS * HD), ENC ** -0.5, 0.1875, ((1, 8),))
    owners_keys = jax.random.split(jax.random.fold_in(splits[5], 1), SPANS // CH_DEV)
    owners_turns = jax.random.permutation(jax.random.fold_in(splits[5], 3), SPANS // CH_DEV)
    owners = jax.vmap(lambda own, number: assign_block(jax.random.fold_in(splits[5], 2), own, number, CH_DEV, N_DP, 2, CAP, 2))(owners_keys, owners_turns).reshape((SPANS, 2))
    slots = plant(jax.random.randint(splits[6], (SPANS, 2), 0, SLABS_DEV), jax.random.fold_in(splits[6], 1), 0, SLABS_DEV - 1).astype(jnp.int32)
    return {"queries": queries, "cotangent": cotangent, "table": table, "key_weight": key_weight, "value_weight": value_weight, "owners": owners, "slots": slots}


def reference(queries, cotangent, table, key_weight, value_weight, owners, slots):
    slab_ids = (owners * SLABS_DEV + slots).astype(jnp.int32)
    kv_width = HEADS * HD
    score_scale = 1.0 / math.sqrt(HD)
    query_spans = queries.reshape(SPANS, SPAN, kv_width)
    grad_spans = cotangent.reshape(SPANS, SPAN, kv_width)

    def per_span(inputs):
        query_rows, grad_rows, span_ids = inputs
        neighbours = table[span_ids].reshape(2 * NLEN, ENC)
        keys = jnp.dot(neighbours, key_weight, preferred_element_type=jnp.float32).astype(jnp.bfloat16)
        values = jnp.dot(neighbours, value_weight, preferred_element_type=jnp.float32).astype(jnp.bfloat16)
        query_f = query_rows.astype(jnp.float32).reshape(SPAN, HEADS, HD)
        grad_f = grad_rows.astype(jnp.float32).reshape(SPAN, HEADS, HD)
        keys_f = keys.astype(jnp.float32).reshape(2 * NLEN, HEADS, HD)
        values_f = values.astype(jnp.float32).reshape(2 * NLEN, HEADS, HD)
        scores = jnp.einsum('qhd,khd->hqk', query_f, keys_f) * score_scale
        attn_probs = jax.nn.softmax(scores, axis=-1)
        weights = attn_probs.astype(jnp.bfloat16).astype(jnp.float32)
        attended = jnp.einsum('hqk,khd->qhd', weights, values_f).astype(jnp.bfloat16).reshape(SPAN, kv_width)
        d_weights = jnp.einsum('qhd,khd->hqk', grad_f, values_f)
        row_sums = lax.optimization_barrier(jnp.sum(d_weights * attn_probs, axis=-1, keepdims=True))
        dscores = (attn_probs * (d_weights - row_sums) * score_scale).astype(jnp.bfloat16).astype(jnp.float32)
        d_query = jnp.einsum('hqk,khd->qhd', dscores, keys_f).astype(jnp.bfloat16).reshape(SPAN, kv_width)
        d_keys = jnp.einsum('hqk,qhd->khd', dscores, query_f).astype(jnp.bfloat16).reshape(2 * NLEN, kv_width)
        d_values = jnp.einsum('hqk,qhd->khd', weights, grad_f).astype(jnp.bfloat16).reshape(2 * NLEN, kv_width)
        d_neigh = jnp.dot(d_keys, key_weight.T, preferred_element_type=jnp.float32)
        d_neigh = d_neigh + jnp.dot(d_values, value_weight.T, preferred_element_type=jnp.float32)
        return (attended, d_query, d_neigh.reshape(2, NLEN, ENC))
    attended, d_query, d_neigh = lax.map(per_span, (query_spans, grad_spans, slab_ids))
    d_table = jnp.zeros((SLABS, NLEN, ENC), jnp.float32).at[slab_ids.reshape(-1)].add(d_neigh.reshape(-1, NLEN, ENC))
    return (attended.reshape(TOKENS, kv_width), d_query.reshape(TOKENS, kv_width), d_table)
```

```python
import functools
import math

import jax
import jax.numpy as jnp
from jax import lax
from jax.experimental import pallas as pl
from jax.experimental.pallas import tpu as pltpu
from jax.sharding import PartitionSpec as P

HD = 128
SPAN = 64
LANES = 128
MESH = pl.DeviceIdType.MESH
VMEM_LIMIT = 48 * 1024 * 1024


def cut_lanes(width, small_last):
    cuts = []
    at = 0
    widths = [256] * (width // 256) + ([width % 256] if width % 256 else [])
    if not small_last:
        widths = widths[::-1]
    for w in widths:
        cuts.append((at, w))
        at += w
    return cuts


def greet(me, t, n_dp, n_x):
    x, core = lax.div(t, 2), lax.rem(t, 2)
    barrier = pltpu.get_barrier_semaphore()

    def hello(i, carry):
        pl.semaphore_signal(
            barrier, inc=1, device_id=(lax.rem(me + i, n_dp), t), device_id_type=MESH
        )
        return carry

    lax.fori_loop(1, n_dp, hello, 0)
    for i in range(1, n_x):
        pl.semaphore_signal(
            barrier,
            inc=1,
            device_id=(me, lax.rem(x + i, n_x) * 2 + core),
            device_id_type=MESH,
        )
    pl.semaphore_signal(barrier, inc=1, device_id=(me, x * 2 + 1 - core), device_id_type=MESH)
    pl.semaphore_wait(barrier, n_dp - 1 + n_x - 1 + 1)


def fetch_kernel(n_dp, n_tp, cuts, owners, slots, table, nb, met, *scratch):
    nk = len(cuts)
    share, send, row, met_s = scratch[:4]
    recv = scratch[4 : 4 + nk]
    sel = scratch[4 + nk : 4 + 2 * nk]
    ld_sem, meta_send, meta_recv, a_send, a_recv, x_send, x_recv, m_send, m_recv = scratch[
        4 + 2 * nk :
    ]
    me = lax.axis_index("dp")
    t = lax.axis_index("tensor")
    n_x = n_tp // 2
    x, core = lax.div(t, 2), lax.rem(t, 2)
    mate = x * 2 + 1 - core
    ts = share.shape[1]
    n_req = 2 * owners.shape[0]

    load = pltpu.make_async_copy(table.at[:, pl.ds(t * ts, ts), :], share, ld_sem)
    load.start()

    lane = lax.broadcasted_iota(jnp.int32, (1, LANES), 1)
    lane_dp = lane & (n_dp - 1)
    lane_place = lax.shift_right_logical(lane, int(math.log2(n_dp))) & 1
    is_slot = lane < 2 * n_dp
    asked_row = jnp.full((1, LANES), -1, jnp.int32)
    seen = jnp.zeros((1, LANES), jnp.int32)
    places = []
    own = [owners[r // 2, r % 2] for r in range(n_req)]
    for r in range(n_req):
        hit = lane_dp == own[r]
        asked_row = jnp.where(
            hit & (seen == lane_place), jnp.where(is_slot, slots[r // 2, r % 2], r), asked_row
        )
        seen = seen + hit.astype(jnp.int32)
        before = jnp.int32(0)
        for other in range(r):
            before = before + jnp.where(own[other] == own[r], 1, 0)
        places.append(2 * own[r] + before)
    row[...] = asked_row

    greet(me, t, n_dp, n_x)

    def meta_copy(peer, slot, sem_slot):
        return pltpu.make_async_remote_copy(
            src_ref=row,
            dst_ref=met.at[slot],
            send_sem=meta_send.at[peer],
            recv_sem=meta_recv.at[sem_slot],
            device_id=(peer, t),
            device_id_type=MESH,
        )

    def start_meta(i, carry):
        meta_copy(lax.rem(me + i, n_dp), me, me).start()
        return carry

    lax.fori_loop(1, n_dp, start_meta, 0)
    met[me] = asked_row

    def wait_meta(i, carry):
        peer = lax.rem(me + i, n_dp)
        meta_copy(peer, peer, peer).wait_recv()
        meta_copy(peer, me, me).wait_send()
        return carry

    lax.fori_loop(1, n_dp, wait_meta, 0)
    to_smem = pltpu.make_async_copy(met, met_s, ld_sem)
    load.wait()
    to_smem.start()
    to_smem.wait()

    def pair_copy(k, peer, slot):
        lo, w = cuts[k]
        return pltpu.make_async_remote_copy(
            src_ref=send.at[pl.ds(2 * peer, 2), :, pl.ds(lo, w)],
            dst_ref=recv[k].at[pl.ds(2 * slot, 2)],
            send_sem=a_send.at[k, peer],
            recv_sem=a_recv.at[k, slot],
            device_id=(peer, t),
            device_id_type=MESH,
        )

    for k, (lo, w) in enumerate(cuts):
        def start_pair(i, carry, k=k, lo=lo, w=w):
            peer = lax.rem(me + i, n_dp)
            for c in range(2):
                index = jnp.maximum(met_s[peer, 0, c * n_dp + me], 0)
                send[2 * peer + c, :, lo : lo + w] = share[index, :, lo : lo + w]
            pair_copy(k, peer, me).start()
            return carry

        lax.fori_loop(1, n_dp, start_pair, 0)
        for c in range(2):
            index = jnp.maximum(met_s[me, 0, c * n_dp + me], 0)
            recv[k][2 * me + c] = share[index, :, lo : lo + w]

    def tensor_copy(k, src, owner_t, peer_t, send_sem, recv_sem):
        lo, w = cuts[k]
        return pltpu.make_async_remote_copy(
            src_ref=src,
            dst_ref=nb.at[:, pl.ds(owner_t * ts, ts), pl.ds(lo, w)],
            send_sem=send_sem,
            recv_sem=recv_sem,
            device_id=(me, peer_t),
            device_id_type=MESH,
        )

    def forward(k):
        lo, w = cuts[k]
        for i in range(1, n_x):
            far = lax.rem(x + n_x - i, n_x) * 2 + core
            tensor_copy(k, sel[k], far, far, x_send.at[k, i], x_recv.at[k, i]).wait_recv()
            tensor_copy(
                k,
                nb.at[:, pl.ds(far * ts, ts), pl.ds(lo, w)],
                far,
                mate,
                m_send.at[k, i],
                m_recv.at[k, i],
            ).start()

    for k, (lo, w) in enumerate(cuts):
        def wait_pair(i, carry, k=k):
            peer = lax.rem(me + i, n_dp)
            pair_copy(k, peer, peer).wait_recv()
            return carry

        lax.fori_loop(1, n_dp, wait_pair, 0)
        for r in range(n_req):
            sel[k][r] = recv[k][places[r]]
        for i in range(1, n_x):
            near = lax.rem(x + i, n_x) * 2 + core
            tensor_copy(k, sel[k], t, near, x_send.at[k, i], x_recv.at[k, i]).start()
        tensor_copy(k, sel[k], t, mate, m_send.at[k, 0], m_recv.at[k, 0]).start()
        nb[:, pl.ds(pl.multiple_of(t * ts, ts), ts), lo : lo + w] = sel[k][...]
        if k > 0:
            forward(k - 1)
    forward(nk - 1)

    for k, (lo, w) in enumerate(cuts):
        for i in range(n_x):
            far = lax.rem(x + n_x - i, n_x) * 2
            tensor_copy(
                k, sel[k], far + 1 - core, mate, m_send.at[k, i], m_recv.at[k, i]
            ).wait_recv()
            tensor_copy(k, sel[k], far + core, mate, m_send.at[k, i], m_recv.at[k, i]).wait_send()
            if i > 0:
                tensor_copy(
                    k, sel[k], t, mate, x_send.at[k, i], x_recv.at[k, i]
                ).wait_send()

        def drain(i, carry, k=k):
            pair_copy(k, lax.rem(me + i, n_dp), me).wait_send()
            return carry

        lax.fori_loop(1, n_dp, drain, 0)


def fetch(n_dp, n_tp, owners, slots, table):
    n_slabs, n_tokens, enc = table.shape
    ts = n_tokens // n_tp
    n_req = 2 * owners.shape[0]
    n_x = n_tp // 2
    cuts = cut_lanes(enc, True)
    nk = len(cuts)
    dma = pltpu.SemaphoreType.DMA
    return pl.pallas_call(
        functools.partial(fetch_kernel, n_dp, n_tp, cuts),
        out_shape=[
            jax.ShapeDtypeStruct((n_req, n_tokens, enc), table.dtype),
            jax.ShapeDtypeStruct((n_dp, 1, LANES), jnp.int32),
        ],
        in_specs=[
            pl.BlockSpec(memory_space=pltpu.SMEM),
            pl.BlockSpec(memory_space=pltpu.SMEM),
            pl.BlockSpec(memory_space=pl.ANY),
        ],
        out_specs=[
            pl.BlockSpec(memory_space=pltpu.VMEM),
            pl.BlockSpec(memory_space=pltpu.VMEM),
        ],
        scratch_shapes=[
            pltpu.VMEM((n_slabs, ts, enc), table.dtype),
            pltpu.VMEM((2 * n_dp, ts, enc), table.dtype),
            pltpu.VMEM((1, LANES), jnp.int32),
            pltpu.SMEM((n_dp, 1, LANES), jnp.int32),
        ]
        + [pltpu.VMEM((2 * n_dp, ts, w), table.dtype) for _, w in cuts]
        + [pltpu.VMEM((n_req, ts, w), table.dtype) for _, w in cuts]
        + [
            dma,
            dma((n_dp,)),
            dma((n_dp,)),
            dma((nk, n_dp)),
            dma((nk, n_dp)),
            dma((nk, n_x)),
            dma((nk, n_x)),
            dma((nk, n_x)),
            dma((nk, n_x)),
        ],
        compiler_params=pltpu.CompilerParams(
            collective_id=0, has_side_effects=True, vmem_limit_bytes=VMEM_LIMIT
        ),
        name="fetch",
    )(owners, slots, table)


def nt(a, b):
    return lax.dot_general(a, b, (((1,), (1,)), ((), ())), preferred_element_type=jnp.float32)


def tn(a, b):
    return lax.dot_general(a, b, (((0,), (0,)), ((), ())), preferred_element_type=jnp.float32)


def nn(a, b):
    return lax.dot_general(a, b, (((1,), (0,)), ((), ())), preferred_element_type=jnp.float32)


def attend_kernel(n_tp, q_ref, g_ref, nb_ref, wk_ref, wv_ref, att_ref, dq_ref, dn_ref):
    bf16 = jnp.bfloat16
    n_tokens, enc = nb_ref.shape[1:]
    ts = n_tokens // n_tp
    scale = 1.0 / math.sqrt(HD)
    width = q_ref.shape[1]
    heads = width // HD
    rows = nb_ref[...].reshape(2 * n_tokens, enc)
    keys = nn(rows, wk_ref[...]).astype(bf16)
    values = nn(rows, wv_ref[...]).astype(bf16)
    q = q_ref[...]
    g = g_ref[...]
    cut = [slice(h * HD, (h + 1) * HD) for h in range(heads)]
    scores = jnp.concatenate([nt(q[:, s], keys[:, s]) for s in cut], axis=0) * scale
    d_weights = jnp.concatenate([nt(g[:, s], values[:, s]) for s in cut], axis=0)
    e = jnp.exp(scores - jnp.max(scores, axis=1, keepdims=True))
    probs = e / jnp.sum(e, axis=1, keepdims=True)
    row_sums = jnp.sum(d_weights * probs, axis=1, keepdims=True)
    ds = (probs * (d_weights - row_sums) * scale).astype(bf16)
    weights = probs.astype(bf16)
    d_keys = []
    d_values = []
    for h, s in enumerate(cut):
        w_h = weights[h * SPAN : (h + 1) * SPAN]
        ds_h = ds[h * SPAN : (h + 1) * SPAN]
        att_ref[:, s] = nn(w_h, values[:, s]).astype(bf16)
        dq_ref[:, s] = nn(ds_h, keys[:, s]).astype(bf16)
        d_keys.append(tn(ds_h, q[:, s]).astype(bf16))
        d_values.append(tn(w_h, g[:, s]).astype(bf16))
    dn = nt(jnp.concatenate(d_keys, axis=1), wk_ref[...])
    dn = dn + nt(jnp.concatenate(d_values, axis=1), wv_ref[...])
    dn = dn.astype(bf16)
    for rr in range(2):
        for t in range(n_tp):
            at = rr * n_tokens + t * ts
            dn_ref[t % 2, t // 2, rr] = dn[at : at + ts]


def attend(n_tp, queries, cotangent, nb, key_weight, value_weight):
    n_req, n_tokens, enc = nb.shape
    spans = n_req // 2
    width = queries.shape[1]
    ts = n_tokens // n_tp
    whole = lambda c: (0, 0)
    return pl.pallas_call(
        functools.partial(attend_kernel, n_tp),
        grid=(spans,),
        out_shape=[
            jax.ShapeDtypeStruct(queries.shape, jnp.bfloat16),
            jax.ShapeDtypeStruct(queries.shape, jnp.bfloat16),
            jax.ShapeDtypeStruct((2, n_tp // 2, n_req, ts, enc), jnp.bfloat16),
        ],
        in_specs=[
            pl.BlockSpec((SPAN, width), lambda c: (c, 0)),
            pl.BlockSpec((SPAN, width), lambda c: (c, 0)),
            pl.BlockSpec((2, n_tokens, enc), lambda c: (c, 0, 0)),
            pl.BlockSpec(key_weight.shape, whole),
            pl.BlockSpec(value_weight.shape, whole),
        ],
        out_specs=[
            pl.BlockSpec((SPAN, width), lambda c: (c, 0)),
            pl.BlockSpec((SPAN, width), lambda c: (c, 0)),
            pl.BlockSpec((2, n_tp // 2, 2, ts, enc), lambda c: (0, 0, c, 0, 0)),
        ],
        compiler_params=pltpu.CompilerParams(vmem_limit_bytes=VMEM_LIMIT),
        name="attend",
    )(queries, cotangent, nb, key_weight, value_weight)


def give_back_kernel(n_dp, n_tp, cuts, met, dn, got, *scratch):
    nk = len(cuts)
    mrecv = scratch[:nk]
    chip = scratch[nk : 2 * nk]
    xrecv = scratch[2 * nk : 3 * nk]
    total = scratch[3 * nk : 4 * nk]
    send = scratch[4 * nk : 5 * nk]
    a_send, a_recv, x_send, x_recv, m_send, m_recv = scratch[5 * nk :]
    me = lax.axis_index("dp")
    t = lax.axis_index("tensor")
    n_x = n_tp // 2
    x, core = lax.div(t, 2), lax.rem(t, 2)
    mate = x * 2 + 1 - core
    n_req = dn.shape[2]

    greet(me, t, n_dp, n_x)

    def mate_copy(k):
        lo, w = cuts[k]
        return pltpu.make_async_remote_copy(
            src_ref=dn.at[1 - core, :, :, :, pl.ds(lo, w)],
            dst_ref=mrecv[k],
            send_sem=m_send.at[k],
            recv_sem=m_recv.at[k],
            device_id=(me, mate),
            device_id_type=MESH,
        )

    def x_copy(k, i):
        far = lax.rem(x + i, n_x)
        return pltpu.make_async_remote_copy(
            src_ref=chip[k].at[far],
            dst_ref=xrecv[k].at[i - 1],
            send_sem=x_send.at[k, i],
            recv_sem=x_recv.at[k, i],
            device_id=(me, far * 2 + core),
            device_id_type=MESH,
        )

    def pair_copy(k, peer, slot):
        lo, w = cuts[k]
        return pltpu.make_async_remote_copy(
            src_ref=send[k].at[pl.ds(2 * peer, 2)],
            dst_ref=got.at[pl.ds(2 * slot, 2), :, pl.ds(lo, w)],
            send_sem=a_send.at[k, peer],
            recv_sem=a_recv.at[k, slot],
            device_id=(peer, t),
            device_id_type=MESH,
        )

    for k in range(nk):
        mate_copy(k).start()

    def pair_sum(k):
        lo, w = cuts[k]
        mate_copy(k).wait_recv()

        def add_rows(j, carry):
            for to in range(n_x):
                both = dn[core, to, j, :, lo : lo + w].astype(jnp.float32) + mrecv[k][
                    to, j
                ].astype(jnp.float32)
                chip[k][to, j] = both.astype(jnp.bfloat16)
            return carry

        lax.fori_loop(0, n_req, add_rows, 0)
        for i in range(1, n_x):
            x_copy(k, i).start()

    def scatter(k):
        lo, w = cuts[k]
        for i in range(1, n_x):
            x_copy(k, i).wait_recv()

        def add_rows(j, carry):
            sum_f = chip[k][x, j].astype(jnp.float32)
            for i in range(1, n_x):
                sum_f = sum_f + xrecv[k][i - 1, j].astype(jnp.float32)
            total[k][j] = sum_f.astype(jnp.bfloat16)
            return carry

        lax.fori_loop(0, n_req, add_rows, 0)

        def start_pair(i, carry):
            peer = lax.rem(me + i, n_dp)
            for c in range(2):
                index = jnp.maximum(met[me, 0, (2 + c) * n_dp + peer], 0)
                send[k][2 * peer + c] = total[k][index]
            pair_copy(k, peer, me).start()
            return carry

        lax.fori_loop(1, n_dp, start_pair, 0)
        for c in range(2):
            index = jnp.maximum(met[me, 0, (2 + c) * n_dp + me], 0)
            got[2 * me + c, :, lo : lo + w] = total[k][index]

    pair_sum(0)
    for k in range(nk):
        if k + 1 < nk:
            pair_sum(k + 1)
        scatter(k)

    for k in range(nk):
        mate_copy(k).wait_send()
        for i in range(1, n_x):
            x_copy(k, i).wait_send()

        def drain(i, carry, k=k):
            peer = lax.rem(me + i, n_dp)
            pair_copy(k, peer, me).wait_send()
            pair_copy(k, peer, peer).wait_recv()
            return carry

        lax.fori_loop(1, n_dp, drain, 0)


def give_back(n_dp, n_tp, met, dn):
    _, n_x, n_req, ts, enc = dn.shape
    cuts = cut_lanes(enc, False)
    nk = len(cuts)
    dma = pltpu.SemaphoreType.DMA
    bf16 = jnp.bfloat16
    return pl.pallas_call(
        functools.partial(give_back_kernel, n_dp, n_tp, cuts),
        out_shape=jax.ShapeDtypeStruct((2 * n_dp, ts, enc), bf16),
        in_specs=[
            pl.BlockSpec(memory_space=pltpu.SMEM),
            pl.BlockSpec(memory_space=pltpu.VMEM),
        ],
        out_specs=pl.BlockSpec(memory_space=pltpu.VMEM),
        scratch_shapes=[pltpu.VMEM((n_x, n_req, ts, w), bf16) for _, w in cuts]
        + [pltpu.VMEM((n_x, n_req, ts, w), bf16) for _, w in cuts]
        + [pltpu.VMEM((n_x - 1, n_req, ts, w), bf16) for _, w in cuts]
        + [pltpu.VMEM((n_req, ts, w), bf16) for _, w in cuts]
        + [pltpu.VMEM((2 * n_dp, ts, w), bf16) for _, w in cuts]
        + [
            dma((nk, n_dp)),
            dma((nk, n_dp)),
            dma((nk, n_x)),
            dma((nk, n_x)),
            dma((nk,)),
            dma((nk,)),
        ],
        compiler_params=pltpu.CompilerParams(
            collective_id=1, has_side_effects=True, vmem_limit_bytes=VMEM_LIMIT
        ),
        name="give_back",
    )(met, dn)


def collect_kernel(n_dp, met, got, out):
    me = lax.axis_index("dp")
    out[...] = jnp.zeros(out.shape, jnp.float32)

    def add(p, carry):
        for c in range(2):
            slab = met[p, 0, c * n_dp + me]

            @pl.when(slab >= 0)
            def _():
                out[slab] = out[slab] + got[2 * p + c].astype(jnp.float32)

        return carry

    lax.fori_loop(0, n_dp, add, 0)


def collect(n_dp, n_slabs, met, got):
    _, ts, enc = got.shape
    return pl.pallas_call(
        functools.partial(collect_kernel, n_dp),
        out_shape=jax.ShapeDtypeStruct((n_slabs, ts, enc), jnp.float32),
        in_specs=[
            pl.BlockSpec(memory_space=pltpu.SMEM),
            pl.BlockSpec(memory_space=pltpu.VMEM),
        ],
        out_specs=pl.BlockSpec(memory_space=pltpu.VMEM),
        name="collect",
    )(met, got)


def on_device(queries, cotangent, table, key_weight, value_weight, owners, slots):
    n_dp = lax.axis_size("dp")
    n_tp = lax.axis_size("tensor")
    nb, met = fetch(n_dp, n_tp, owners, slots, table)
    attended, d_query, dn = attend(n_tp, queries, cotangent, nb, key_weight, value_weight)
    got = give_back(n_dp, n_tp, met, dn)
    d_table = collect(n_dp, table.shape[0], met, got)
    return (attended, d_query, d_table)


def solution(mesh):
    in_specs = (
        P("dp", "tensor"),
        P("dp", "tensor"),
        P("dp", None, None),
        P(None, "tensor"),
        P(None, "tensor"),
        P("dp", None),
        P("dp", None),
    )
    out_specs = (P("dp", "tensor"), P("dp", "tensor"), P("dp", "tensor", None))
    return jax.shard_map(
        on_device, mesh=mesh, in_specs=in_specs, out_specs=out_specs, check_vma=False
    )
```

```python
import functools
import math

import jax
import jax.numpy as jnp
from jax import lax
from jax.experimental import pallas as pl
from jax.experimental.pallas import tpu as pltpu
from jax.sharding import PartitionSpec as P

HD = 128
SPAN = 64
LANES = 128
N_Y = 4
N_Z = 8
HOPS = 6
LAG = 3
AHEAD = 4
FWD_GROUPS = ((6, 2), (5, 3), (4,), (1, 7, 0))
BWD_GROUPS = ((0, 1, 7), (4,), (3, 5), (2, 6))
BWD_READY = {1: 0, 4: 1, 5: 2, 6: 3}
MESH = pl.DeviceIdType.MESH
VMEM_LIMIT = 56 * 1024 * 1024


def lane_chunks(enc):
    units = enc // LANES
    first = (units + 1) // 2
    chunks = []
    at = 0
    for half, count in ((0, first), (1, units - first)):
        for n in ((count + 1) // 2, count // 2):
            if n:
                chunks.append((at * LANES, n * LANES, half))
                at += n
    return chunks


def ring_order(chunks, last):
    ops = [(s, k) for s in range(1, last + 1) for k in range(len(chunks))]
    return sorted(ops, key=lambda o: (o[0] + LAG * chunks[o[1]][2], chunks[o[1]][2], o[1]))


def find_group(groups, d):
    for g, members in enumerate(groups):
        if d in members:
            return g, members.index(d)


def nt(a, b):
    return lax.dot_general(a, b, (((1,), (1,)), ((), ())), preferred_element_type=jnp.float32)


def tn(a, b):
    return lax.dot_general(a, b, (((0,), (0,)), ((), ())), preferred_element_type=jnp.float32)


def nn(a, b):
    return lax.dot_general(a, b, (((1,), (0,)), ((), ())), preferred_element_type=jnp.float32)


def span_grads(q, g, rows, wk, wv):
    bf16 = jnp.bfloat16
    scale = 1.0 / math.sqrt(HD)
    heads = q.shape[1] // HD
    keys = nn(rows, wk).astype(bf16)
    values = nn(rows, wv).astype(bf16)
    cut = [slice(h * HD, (h + 1) * HD) for h in range(heads)]
    scores = jnp.concatenate([nt(q[:, s], keys[:, s]) for s in cut], axis=0) * scale
    d_weights = jnp.concatenate([nt(g[:, s], values[:, s]) for s in cut], axis=0)
    e = jnp.exp(scores - jnp.max(scores, axis=1, keepdims=True))
    probs = e / jnp.sum(e, axis=1, keepdims=True)
    row_sums = jnp.sum(d_weights * probs, axis=1, keepdims=True)
    ds = (probs * (d_weights - row_sums) * scale).astype(bf16)
    weights = probs.astype(bf16)
    attended, d_query, d_keys, d_values = [], [], [], []
    for h, s in enumerate(cut):
        w_h = weights[h * SPAN : (h + 1) * SPAN]
        ds_h = ds[h * SPAN : (h + 1) * SPAN]
        attended.append(nn(w_h, values[:, s]).astype(bf16))
        d_query.append(nn(ds_h, keys[:, s]).astype(bf16))
        d_keys.append(tn(ds_h, q[:, s]).astype(bf16))
        d_values.append(tn(w_h, g[:, s]).astype(bf16))
    dn = nt(jnp.concatenate(d_keys, axis=1), wk) + nt(jnp.concatenate(d_values, axis=1), wv)
    return (
        jnp.concatenate(attended, axis=1),
        jnp.concatenate(d_query, axis=1),
        dn.astype(bf16),
    )


def fused_kernel(
    n_dp, n_tp, treedef, owners, slots, table, queries, cotangent, key_weight, value_weight, att, dq, dt, *flat
):
    b = jax.tree_util.tree_unflatten(treedef, flat)
    bf16 = jnp.bfloat16
    me = lax.axis_index("dp")
    t = lax.axis_index("tensor")
    z, y = lax.div(me, N_Y), lax.rem(me, N_Y)
    n_x = n_tp // 2
    x, core = lax.div(t, 2), lax.rem(t, 2)
    mate = x * 2 + 1 - core
    n_req, ts, enc = b["sel"].shape
    spans = n_req // 2
    side = n_req // 2
    n_tokens = ts * n_tp
    chunks = lane_chunks(enc)
    nk = len(chunks)
    first_w = sum(w for _, w, half in chunks if half == 0)
    halves = ((0, first_w), (first_w, enc - first_w))

    def up(d):
        return lax.rem(z + d, N_Z)

    def send_to(src, dst, ss, rs, dp_to, t_to):
        return pltpu.make_async_remote_copy(
            src_ref=src, dst_ref=dst, send_sem=ss, recv_sem=rs, device_id=(dp_to, t_to), device_id_type=MESH
        )

    loads = [
        pltpu.make_async_copy(table.at[:, pl.ds(t * ts, ts), :], b["share"], b["load_sem"].at[0]),
        pltpu.make_async_copy(key_weight, b["wk"], b["load_sem"].at[1]),
        pltpu.make_async_copy(value_weight, b["wv"], b["load_sem"].at[2]),
        pltpu.make_async_copy(queries, b["q"], b["load_sem"].at[3]),
        pltpu.make_async_copy(cotangent, b["g"], b["load_sem"].at[4]),
    ]
    for load in loads:
        load.start()

    barrier = pltpu.get_barrier_semaphore()
    peers = (
        [(up(d) * N_Y + y, t) for d in range(1, N_Z)]
        + [(z * N_Y + lax.rem(y + i, N_Y), t) for i in range(1, N_Y)]
        + [(me, lax.rem(x + i, n_x) * 2 + core) for i in range(1, n_x)]
        + [(me, mate)]
    )
    for peer in peers:
        pl.semaphore_signal(barrier, inc=1, device_id=peer, device_id_type=MESH)

    lane = lax.broadcasted_iota(jnp.int32, (1, LANES), 1)
    lane_dp = lane & (n_dp - 1)
    lane_place = lax.shift_right_logical(lane, int(math.log2(n_dp))) & 1
    is_slot = lane < 2 * n_dp
    own = [owners[r % 2, r // 2] for r in range(n_req)]
    far = [lax.rem(z - lax.div(own[r], N_Y) + N_Z, N_Z) for r in range(n_req)]
    key = [jnp.where(far[r] == 0, N_Z // 2, far[r]) for r in range(n_req)]
    asked_row = jnp.full((1, LANES), -1, jnp.int32)
    list_row = jnp.zeros((1, LANES), jnp.int32)
    seen = jnp.zeros((1, LANES), jnp.int32)
    ranks = []
    for r in range(n_req):
        before = jnp.int32(0)
        rank = jnp.int32(0)
        for other in range(n_req):
            if other < r:
                before = before + jnp.where(own[other] == own[r], 1, 0)
                rank = rank + jnp.where(key[other] <= key[r], 1, 0)
            elif other > r:
                rank = rank + jnp.where(key[other] < key[r], 1, 0)
        ranks.append(rank)
        hit = lane_dp == own[r]
        asked_row = jnp.where(
            hit & (seen == lane_place), jnp.where(is_slot, slots[r % 2, r // 2], rank), asked_row
        )
        seen = seen + hit.astype(jnp.int32)
        list_row = jnp.where(lane == rank, 2 * own[r] + before, list_row)
        list_row = jnp.where(lane == rank + n_req, r, list_row)
    my_rows = jnp.concatenate([asked_row, list_row], axis=0)
    b["row"][...] = my_rows

    pl.semaphore_wait(barrier, len(peers))

    met, met_s = b["met"], b["met_s"]
    for d in range(1, N_Z):
        send_to(
            b["row"], met.at[y, z], b["meta_send"].at[d], b["meta_recv"].at[d], up(d) * N_Y + y, t
        ).start()
    met[y, z] = my_rows
    for d in range(1, N_Z):
        send_to(
            b["row"], met.at[y, up(N_Z - d)], b["meta_send"].at[d], b["meta_recv"].at[d], up(d) * N_Y + y, t
        ).wait()

    def meta_y(i, from_y):
        return send_to(
            met.at[from_y],
            met.at[from_y],
            b["meta_send"].at[N_Z + i],
            b["meta_recv"].at[N_Z + i],
            z * N_Y + lax.rem(y + i, N_Y),
            t,
        )

    for i in range(1, N_Y):
        meta_y(i, y).start()
    for i in range(1, N_Y):
        meta_y(i, lax.rem(y + N_Y - i, N_Y)).wait_recv()
        meta_y(i, y).wait_send()
    to_smem = pltpu.make_async_copy(met, met_s, b["load_sem"].at[5])
    loads[0].wait()
    to_smem.start()
    to_smem.wait()

    share = b["share"]

    def y_copy(k, g, i, from_y):
        return send_to(
            b["y_out"][k][g].at[i - 1],
            b["cand"][k][g].at[from_y],
            b["y_send"].at[k, g, i],
            b["y_recv"].at[k, g, i],
            z * N_Y + lax.rem(y + i, N_Y),
            t,
        )

    def y_pieces(k, g, to_y):
        lo, w, _ = chunks[k]
        for n, d in enumerate(FWD_GROUPS[g]):
            for c in range(2):
                index = jnp.maximum(met_s[to_y, up(d), 0, c * n_dp + me], 0)
                yield n, c, share[index, :, lo : lo + w]

    def y_build(k, g):
        for i in range(1, N_Y):
            for n, c, piece in y_pieces(k, g, lax.rem(y + i, N_Y)):
                b["y_out"][k][g][i - 1, n, c] = piece
            y_copy(k, g, i, y).start()
        for n, c, piece in y_pieces(k, g, y):
            b["cand"][k][g][y, n, c] = piece

    def ring_copy(k, s, up_way, forward):
        rings, first, ss, rs = (
            (b["ring"], b["first"], b["ring_send"], b["ring_recv"])
            if forward
            else (b["back"], b["lists"], b["back_send"], b["back_recv"])
        )
        from_up = up_way if forward else not up_way
        rows = pl.ds(0 if from_up else side, side)
        src = first[k] if s == 1 else ring_slot(rings, k, s - 1)
        return send_to(
            src.at[rows],
            ring_slot(rings, k, s).at[rows],
            ss.at[k, s, 0 if up_way else 1],
            rs.at[k, s, 0 if up_way else 1],
            up(1 if up_way else N_Z - 1) * N_Y + y,
            t,
        )

    def ring_slot(rings, k, s):
        pair, at = {1: (0, 0), 2: (1, 0), 6: (1, 1), 3: (2, 0), 5: (2, 1), 4: (3, 0)}[s]
        return rings[k][pair].at[at]

    def merge(k, buf, dist, fresh):
        for down in range(2):
            d = (N_Z - dist) % N_Z if down else dist
            g, n = find_group(FWD_GROUPS, d)
            cand = b["cand"][k][g]
            asker = up(d)

            def one(j, carry, down=down, cand=cand, asker=asker, n=n):
                slot = down * side + j
                code = met_s[y, asker, 1, slot]
                mine = cand[lax.rem(lax.div(code, 2), N_Y), n, lax.rem(code, 2)]
                if not fresh:
                    here = lax.div(code, 2 * N_Y) == z
                    mine = jnp.where(here, mine, buf[slot])
                buf[slot] = mine
                return carry

            lax.fori_loop(0, side, one, 0)

    def t_copy(src, owner_t, r0, nr, lo, w, ss, rs, to_t):
        return send_to(
            src, b["nb"].at[pl.ds(r0, nr), pl.ds(owner_t * ts, ts), pl.ds(lo, w)], ss, rs, me, to_t
        )

    def gather_x(u, r0, nr, lo, w, i, from_t):
        return t_copy(
            b["sel"].at[pl.ds(r0, nr), :, pl.ds(lo, w)],
            from_t,
            r0,
            nr,
            lo,
            w,
            b["gx_send"].at[u, i],
            b["gx_recv"].at[u, i],
            lax.rem(x + i, n_x) * 2 + core,
        )

    def gather_mate(u, r0, nr, lo, w, i, from_core):
        from_t = lax.rem(x + n_x - i, n_x) * 2 + from_core
        src = (
            b["sel"].at[pl.ds(r0, nr), :, pl.ds(lo, w)]
            if i == 0
            else b["nb"].at[pl.ds(r0, nr), pl.ds(from_t * ts, ts), pl.ds(lo, w)]
        )
        return t_copy(
            src, from_t, r0, nr, lo, w, b["gm_send"].at[u, i], b["gm_recv"].at[u, i], mate
        )

    def gather_start(u, r0, nr, lo, w):
        for i in range(1, n_x):
            gather_x(u, r0, nr, lo, w, i, t).start()
        gather_mate(u, r0, nr, lo, w, 0, core).start()

    def gather_forward(u, r0, nr, lo, w):
        for i in range(1, n_x):
            gather_x(u, r0, nr, lo, w, i, lax.rem(x + n_x - i, n_x) * 2 + core).wait_recv()
            gather_mate(u, r0, nr, lo, w, i, core).start()

    def gather_arrived(u, r0, nr, lo, w):
        for i in range(n_x):
            gather_mate(u, r0, nr, lo, w, i, 1 - core).wait_recv()

    def gather_sent(u, r0, nr, lo, w):
        for i in range(n_x):
            if i > 0:
                gather_x(u, r0, nr, lo, w, i, t).wait_send()
            gather_mate(u, r0, nr, lo, w, i, core).wait_send()

    unit_a = (spans, 0, n_req, *halves[0])

    def unit_b(c):
        return (c, 2 * c, 2, *halves[1])

    order = ring_order(chunks, HOPS + 1)
    needs = []
    for s, k in order:
        for d in (HOPS + 1 - s, (N_Z - HOPS - 1 + s) % N_Z):
            pair = (k, find_group(FWD_GROUPS, d)[0])
            if pair not in needs:
                needs.append(pair)
    built, landed = 0, []
    finals = [0, 0]
    for at, (s, k) in enumerate(order):
        dist = HOPS + 1 - s
        wanted = []
        for s2, k2 in order[at : at + 1 + AHEAD]:
            wanted.append((k2, find_group(FWD_GROUPS, HOPS + 1 - s2)[0]))
        while any(pair in needs[built:] for pair in wanted):
            y_build(*needs[built])
            built += 1
        if s > 1:
            for up_way in (True, False):
                ring_copy(k, s - 1, up_way, True).wait_recv()
        g = find_group(FWD_GROUPS, dist)[0]
        if (k, g) not in landed:
            for i in range(1, N_Y):
                y_copy(k, g, i, lax.rem(y + N_Y - i, N_Y)).wait_recv()
            landed.append((k, g))
        buf = b["first"][k] if s == 1 else ring_slot(b["ring"], k, s - 1)
        merge(k, buf, dist, s == 1)
        if s <= HOPS:
            for up_way in (True, False):
                ring_copy(k, s, up_way, True).start()
            continue
        lo, w, half = chunks[k]
        for r in range(n_req):
            b["sel"][r, :, lo : lo + w] = buf[ranks[r]]
        finals[half] += 1
        if finals[half] == sum(1 for c in chunks if c[2] == half):
            if half == 0:
                gather_start(*unit_a)
            else:
                for c in range(spans):
                    gather_start(*unit_b(c))
    b["nb"][:, pl.ds(pl.multiple_of(t * ts, ts), ts), :] = b["sel"][...]

    back_order = [d for members in BWD_GROUPS for d in members]
    per = LANES // ts
    lane_tok = lax.rem(lane, ts)
    lane_piece = lax.div(lane, ts)
    tall = lax.broadcasted_iota(jnp.int32, (b["place"].shape[0], LANES), 0)
    for group in range(b["place"].shape[1] // LANES):
        line = jnp.full((1, LANES), -1, jnp.int32)
        for j in range(per):
            piece = group * per + j
            c, pos, from_y = piece % 2, piece // 2 % N_Z, piece // 2 // N_Z
            slab = met_s[from_y, up(back_order[pos]), 0, c * n_dp + me]
            line = jnp.where(lane_piece == j, slab * ts + lane_tok, line)
        b["place"][:, group * LANES : (group + 1) * LANES] = jnp.where(
            tall == line, 1.0, 0.0
        ).astype(bf16)

    for load in loads[1:]:
        load.wait()
    gather_forward(*unit_a)
    gather_forward(*unit_b(0))
    gather_arrived(*unit_a)

    def mate_copy(c):
        rows = pl.ds(2 * c, 2)
        return send_to(
            b["dn"].at[1 - core, :, rows],
            b["from_mate"].at[:, rows],
            b["rm_send"].at[c],
            b["rm_recv"].at[c],
            me,
            mate,
        )

    def x_copy(u, r0, nr, half, i):
        lo, w = halves[half]
        to_x = lax.rem(x + i, n_x)
        return send_to(
            b["chip"].at[to_x, pl.ds(r0, nr), :, pl.ds(lo, w)],
            b["from_x"].at[i - 1, pl.ds(r0, nr), :, pl.ds(lo, w)],
            b["rx_send"].at[u, i],
            b["rx_recv"].at[u, i],
            me,
            to_x * 2 + core,
        )

    def pair_sum(c):
        mate_copy(c).wait_recv()
        rows = pl.ds(2 * c, 2)
        both = b["dn"][core, :, rows].astype(jnp.float32) + b["from_mate"][:, rows].astype(jnp.float32)
        b["chip"][:, rows] = both.astype(bf16)
        for i in range(1, n_x):
            x_copy(c, 2 * c, 2, 0, i).start()

    def span(c, carry):
        @pl.when(c + 1 < spans)
        def _():
            gather_forward(*unit_b(c + 1))

        gather_arrived(*unit_b(c))
        tokens = pl.ds(pl.multiple_of(c * SPAN, SPAN), SPAN)
        rows = b["nb"][pl.ds(2 * c, 2)].reshape(2 * n_tokens, enc)
        att_c, dq_c, dn_c = span_grads(
            b["q"][tokens, :], b["g"][tokens, :], rows, b["wk"][...], b["wv"][...]
        )
        b["att_v"][tokens, :] = att_c
        b["dq_v"][tokens, :] = dq_c
        for rr in range(2):
            for to_t in range(n_tp):
                lo = rr * n_tokens + to_t * ts
                b["dn"][to_t % 2, to_t // 2, 2 * c + rr] = dn_c[lo : lo + ts]
        mate_copy(c).start()

        @pl.when(c >= 1)
        def _():
            pair_sum(c - 1)

        return carry

    lax.fori_loop(0, spans, span, 0)
    stores = [
        pltpu.make_async_copy(b["att_v"], att, b["load_sem"].at[6]),
        pltpu.make_async_copy(b["dq_v"], dq, b["load_sem"].at[7]),
    ]
    for store in stores:
        store.start()
    pair_sum(spans - 1)
    for i in range(1, n_x):
        x_copy(spans, 0, n_req, 1, i).start()

    def back_lists(half):
        lo, w = halves[half]
        if half == 0:

            def landed_x(c, carry):
                for i in range(1, n_x):
                    x_copy(c, 2 * c, 2, 0, i).wait_recv()
                return carry

            lax.fori_loop(0, spans, landed_x, 0)
        else:
            for i in range(1, n_x):
                x_copy(spans, 0, n_req, 1, i).wait_recv()

        def add(j, carry):
            total = b["chip"][x, j, :, lo : lo + w].astype(jnp.float32)
            for i in range(1, n_x):
                total = total + b["from_x"][i - 1, j, :, lo : lo + w].astype(jnp.float32)
            b["total"][half][j] = total.astype(bf16)
            return carry

        lax.fori_loop(0, n_req, add, 0)
        for k, (k_lo, k_w, k_half) in enumerate(chunks):
            if k_half == half:

                def pick(j, carry, k=k, at=k_lo - lo, k_w=k_w):
                    b["lists"][k][j] = b["total"][half][met_s[y, z, 1, n_req + j], :, at : at + k_w]
                    return carry

                lax.fori_loop(0, n_req, pick, 0)

    def yb_copy(k, h, i, from_y):
        at = sum(len(m) for m in BWD_GROUPS[:h])
        return send_to(
            b["yb_out"][k][h].at[i - 1],
            b["got"][k].at[from_y, pl.ds(at, len(BWD_GROUPS[h]))],
            b["yb_send"].at[k, h, i],
            b["yb_recv"].at[k, h, i],
            z * N_Y + lax.rem(y + i, N_Y),
            t,
        )

    def yb_pieces(k, h, to_y):
        for n, d in enumerate(BWD_GROUPS[h]):
            for c in range(2):
                j = met_s[y, up(d), 0, (2 + c) * n_dp + z * N_Y + to_y]
                j = jnp.minimum(jnp.maximum(j, 0), n_req - 1)
                if d == 0:
                    piece = b["lists"][k][j]
                elif d in (1, 7, 4):
                    piece = b["back"][k][0 if d != 4 else 3][0, j]
                else:
                    early = jnp.where(j < side, d, N_Z - d) < 4
                    piece = b["back"][k][1 if d in (2, 6) else 2][jnp.where(early, 0, 1), j]
                yield n, c, piece

    def yb_build(k, h):
        at = sum(len(m) for m in BWD_GROUPS[:h])
        for i in range(1, N_Y):
            for n, c, piece in yb_pieces(k, h, lax.rem(y + i, N_Y)):
                b["yb_out"][k][h][i - 1, n, c] = piece
            yb_copy(k, h, i, y).start()
        for n, c, piece in yb_pieces(k, h, y):
            b["got"][k][y, at + n, c] = piece

    listed = [False, False]
    for s, k in ring_order(chunks, HOPS + 1):
        half = chunks[k][2]
        if not listed[half]:
            back_lists(half)
            listed[half] = True
        if s > 1:
            for up_way in (True, False):
                ring_copy(k, s - 1, up_way, False).wait_recv()
        if s <= HOPS:
            for up_way in (True, False):
                ring_copy(k, s, up_way, False).start()
        if s - 1 in BWD_READY:
            yb_build(k, BWD_READY[s - 1])

    for k, (lo, w, _) in enumerate(chunks):
        for h in range(len(BWD_GROUPS)):
            for i in range(1, N_Y):
                yb_copy(k, h, i, lax.rem(y + N_Y - i, N_Y)).wait_recv()
        pieces = b["got"][k][...].reshape(b["place"].shape[1], w)
        dt[:, :, lo : lo + w] = nn(b["place"][...], pieces).reshape(dt.shape[0], ts, w)

    for store in stores:
        store.wait()
    for k in range(nk):
        for g in range(len(FWD_GROUPS)):
            for i in range(1, N_Y):
                y_copy(k, g, i, y).wait_send()
                yb_copy(k, g, i, y).wait_send()
        for s in range(1, HOPS + 1):
            for up_way in (True, False):
                ring_copy(k, s, up_way, True).wait_send()
                ring_copy(k, s, up_way, False).wait_send()
    gather_sent(*unit_a)
    for i in range(1, n_x):
        x_copy(spans, 0, n_req, 1, i).wait_send()

    def drain(c, carry):
        gather_sent(*unit_b(c))
        mate_copy(c).wait_send()
        for i in range(1, n_x):
            x_copy(c, 2 * c, 2, 0, i).wait_send()
        return carry

    lax.fori_loop(0, spans, drain, 0)


def on_device(queries, cotangent, table, key_weight, value_weight, owners, slots):
    n_dp = lax.axis_size("dp")
    n_tp = lax.axis_size("tensor")
    n_slabs, n_tokens, enc = table.shape
    ts = n_tokens // n_tp
    spans = owners.shape[0]
    n_req = 2 * spans
    n_x = n_tp // 2
    side = n_req // 2
    chunks = lane_chunks(enc)
    nk = len(chunks)
    first_w = sum(w for _, w, half in chunks if half == 0)
    dma = pltpu.SemaphoreType.DMA
    bf16 = jnp.bfloat16
    vm = lambda *shape: pltpu.VMEM(shape, bf16)
    ng = len(FWD_GROUPS)
    rings = lambda w: [vm(n, n_req, ts, w) for n in (1, 2, 2, 1)]
    scratch = dict(
        share=vm(n_slabs, ts, enc),
        wk=vm(*key_weight.shape),
        wv=vm(*value_weight.shape),
        q=vm(*queries.shape),
        g=vm(*cotangent.shape),
        att_v=vm(*queries.shape),
        dq_v=vm(*queries.shape),
        row=pltpu.VMEM((2, LANES), jnp.int32),
        met=pltpu.VMEM((N_Y, N_Z, 2, LANES), jnp.int32),
        met_s=pltpu.SMEM((N_Y, N_Z, 2, LANES), jnp.int32),
        y_out=[[vm(N_Y - 1, len(m), 2, ts, w) for m in FWD_GROUPS] for _, w, _ in chunks],
        cand=[[vm(N_Y, len(m), 2, ts, w) for m in FWD_GROUPS] for _, w, _ in chunks],
        first=[vm(n_req, ts, w) for _, w, _ in chunks],
        ring=[rings(w) for _, w, _ in chunks],
        sel=vm(n_req, ts, enc),
        nb=vm(n_req, n_tokens, enc),
        place=vm(n_slabs * ts, 2 * n_dp * ts),
        dn=vm(2, n_x, n_req, ts, enc),
        from_mate=vm(n_x, n_req, ts, enc),
        chip=vm(n_x, n_req, ts, enc),
        from_x=vm(max(n_x - 1, 1), n_req, ts, enc),
        total=[vm(n_req, ts, first_w), vm(n_req, ts, enc - first_w)],
        lists=[vm(n_req, ts, w) for _, w, _ in chunks],
        back=[rings(w) for _, w, _ in chunks],
        yb_out=[[vm(N_Y - 1, len(m), 2, ts, w) for m in BWD_GROUPS] for _, w, _ in chunks],
        got=[vm(N_Y, N_Z, 2, ts, w) for _, w, _ in chunks],
        load_sem=dma((8,)),
        meta_send=dma((N_Z + N_Y,)),
        meta_recv=dma((N_Z + N_Y,)),
        y_send=dma((nk, ng, N_Y)),
        y_recv=dma((nk, ng, N_Y)),
        yb_send=dma((nk, ng, N_Y)),
        yb_recv=dma((nk, ng, N_Y)),
        ring_send=dma((nk, HOPS + 1, 2)),
        ring_recv=dma((nk, HOPS + 1, 2)),
        back_send=dma((nk, HOPS + 1, 2)),
        back_recv=dma((nk, HOPS + 1, 2)),
        gx_send=dma((spans + 1, n_x)),
        gx_recv=dma((spans + 1, n_x)),
        gm_send=dma((spans + 1, n_x)),
        gm_recv=dma((spans + 1, n_x)),
        rm_send=dma((spans,)),
        rm_recv=dma((spans,)),
        rx_send=dma((spans + 1, n_x)),
        rx_recv=dma((spans + 1, n_x)),
    )
    leaves, treedef = jax.tree_util.tree_flatten(scratch)
    anywhere = pl.BlockSpec(memory_space=pl.ANY)
    return pl.pallas_call(
        functools.partial(fused_kernel, n_dp, n_tp, treedef),
        out_shape=[
            jax.ShapeDtypeStruct(queries.shape, bf16),
            jax.ShapeDtypeStruct(queries.shape, bf16),
            jax.ShapeDtypeStruct((n_slabs, ts, enc), jnp.float32),
        ],
        in_specs=[pl.BlockSpec(memory_space=pltpu.SMEM)] * 2 + [anywhere] * 5,
        out_specs=[anywhere, anywhere, pl.BlockSpec(memory_space=pltpu.VMEM)],
        scratch_shapes=leaves,
        compiler_params=pltpu.CompilerParams(
            collective_id=0, has_side_effects=True, vmem_limit_bytes=VMEM_LIMIT
        ),
        name="spanned",
    )(owners.T, slots.T, table, queries, cotangent, key_weight, value_weight)


def solution(mesh):
    in_specs = (
        P("dp", "tensor"),
        P("dp", "tensor"),
        P("dp", None, None),
        P(None, "tensor"),
        P(None, "tensor"),
        P("dp", None),
        P("dp", None),
    )
    out_specs = (P("dp", "tensor"), P("dp", "tensor"), P("dp", "tensor", None))
    return jax.shard_map(
        on_device, mesh=mesh, in_specs=in_specs, out_specs=out_specs, check_vma=False
    )
```

```python
import functools
import math

import jax
import jax.numpy as jnp
from jax import lax
from jax.experimental import pallas as pl
from jax.experimental.pallas import tpu as pltpu
from jax.sharding import PartitionSpec as P

HD = 128
SPAN = 64
LANES = 128
N_Y = 4
N_Z = 8
HOPS = 6
N_X = 4
CHUNKS = 4
AHEAD = 4
GATHER_AHEAD = 8
PASS_AHEAD = 4
FAR_AHEAD = 2
FWD_GROUPS = ((6, 2), (5, 3), (4,), (1, 7, 0))
BWD_GROUPS = ((0, 1, 7), (4,), (3, 5), (2, 6))
BWD_READY = {1: 0, 4: 1, 5: 2, 6: 3}
MESH = pl.DeviceIdType.MESH
VMEM_LIMIT = 56 * 1024 * 1024


def lane_chunks(enc):
    units = enc // LANES
    count = min(CHUNKS, units)
    chunks = []
    at = 0
    for left in range(count, 0, -1):
        n = (units - at) // left
        chunks.append((at * LANES, n * LANES))
        at += n
    return chunks


def ring_order(chunks, last, backward):
    ks = range(len(chunks))
    return [(s, k) for s in range(1, last + 1) for k in (reversed(ks) if backward else ks)]


def find_group(groups, d):
    for g, members in enumerate(groups):
        if d in members:
            return g, members.index(d)


def nt(a, b):
    return lax.dot_general(a, b, (((1,), (1,)), ((), ())), preferred_element_type=jnp.float32)


def tn(a, b):
    return lax.dot_general(a, b, (((0,), (0,)), ((), ())), preferred_element_type=jnp.float32)


def nn(a, b):
    return lax.dot_general(a, b, (((1,), (0,)), ((), ())), preferred_element_type=jnp.float32)


def span_grads(q, g, rows, wk, wv):
    bf16 = jnp.bfloat16
    scale = 1.0 / math.sqrt(HD)
    heads = q.shape[1] // HD
    keys = nn(rows, wk).astype(bf16)
    values = nn(rows, wv).astype(bf16)
    cut = [slice(h * HD, (h + 1) * HD) for h in range(heads)]
    scores = jnp.concatenate([nt(q[:, s], keys[:, s]) for s in cut], axis=0) * scale
    d_weights = jnp.concatenate([nt(g[:, s], values[:, s]) for s in cut], axis=0)
    e = jnp.exp(scores - jnp.max(scores, axis=1, keepdims=True))
    probs = e / jnp.sum(e, axis=1, keepdims=True)
    row_sums = jnp.sum(d_weights * probs, axis=1, keepdims=True)
    ds = (probs * (d_weights - row_sums) * scale).astype(bf16)
    weights = probs.astype(bf16)
    attended, d_query, d_keys, d_values = [], [], [], []
    for h, s in enumerate(cut):
        w_h = weights[h * SPAN : (h + 1) * SPAN]
        ds_h = ds[h * SPAN : (h + 1) * SPAN]
        attended.append(nn(w_h, values[:, s]).astype(bf16))
        d_query.append(nn(ds_h, keys[:, s]).astype(bf16))
        d_keys.append(tn(ds_h, q[:, s]).astype(bf16))
        d_values.append(tn(w_h, g[:, s]).astype(bf16))
    dn = nt(jnp.concatenate(d_keys, axis=1), wk) + nt(jnp.concatenate(d_values, axis=1), wv)
    return (
        jnp.concatenate(attended, axis=1),
        jnp.concatenate(d_query, axis=1),
        dn.astype(bf16),
    )


def fused_kernel(
    n_dp, n_tp, treedef, owners, slots, table, queries, cotangent, key_weight, value_weight, att, dq, dt, *flat
):
    b = jax.tree_util.tree_unflatten(treedef, flat)
    bf16 = jnp.bfloat16
    me = lax.axis_index("dp")
    t = lax.axis_index("tensor")
    z, y = lax.div(me, N_Y), lax.rem(me, N_Y)
    x, core = lax.div(t, 2), lax.rem(t, 2)
    mate = x * 2 + 1 - core
    x_up, x_far, x_down = [lax.rem(x + i, N_X) for i in range(1, N_X)]
    n_req, ts, enc = b["sel"].shape
    spans = n_req // 2
    side = n_req // 2
    n_tokens = ts * n_tp
    chunks = lane_chunks(enc)
    nk = len(chunks)

    def up(d):
        return lax.rem(z + d, N_Z)

    def send_to(src, dst, ss, rs, dp_to, t_to):
        return pltpu.make_async_remote_copy(
            src_ref=src, dst_ref=dst, send_sem=ss, recv_sem=rs, device_id=(dp_to, t_to), device_id_type=MESH
        )

    def landed_all(ref, sem):
        pltpu.make_async_copy(ref, ref, sem).wait()

    loads = [
        pltpu.make_async_copy(table.at[:, pl.ds(t * ts, ts), :], b["share"], b["load_sem"].at[0]),
        pltpu.make_async_copy(key_weight, b["wk"], b["load_sem"].at[1]),
        pltpu.make_async_copy(value_weight, b["wv"], b["load_sem"].at[2]),
        pltpu.make_async_copy(queries, b["q"], b["load_sem"].at[3]),
        pltpu.make_async_copy(cotangent, b["g"], b["load_sem"].at[4]),
    ]
    for load in loads:
        load.start()

    barrier = pltpu.get_barrier_semaphore()
    def hello(i, carry):
        pl.semaphore_signal(
            barrier, inc=1, device_id=(lax.rem(me + i, n_dp), t), device_id_type=MESH
        )
        return carry

    lax.fori_loop(1, n_dp, hello, 0)
    for peer_t in (x_up * 2 + core, x_down * 2 + core, mate):
        pl.semaphore_signal(barrier, inc=1, device_id=(me, peer_t), device_id_type=MESH)

    lane = lax.broadcasted_iota(jnp.int32, (1, LANES), 1)
    lane_dp = lane & (n_dp - 1)
    lane_place = lax.shift_right_logical(lane, int(math.log2(n_dp))) & 1
    is_slot = lane < 2 * n_dp
    own = [owners[r % 2, r // 2] for r in range(n_req)]
    far = [lax.rem(z - lax.div(own[r], N_Y) + N_Z, N_Z) for r in range(n_req)]
    key = [jnp.where(far[r] == 0, N_Z // 2, far[r]) for r in range(n_req)]
    asked_row = jnp.full((1, LANES), -1, jnp.int32)
    list_row = jnp.zeros((1, LANES), jnp.int32)
    seen = jnp.zeros((1, LANES), jnp.int32)
    ranks = []
    for r in range(n_req):
        before = jnp.int32(0)
        rank = jnp.int32(0)
        for other in range(n_req):
            if other < r:
                before = before + jnp.where(own[other] == own[r], 1, 0)
                rank = rank + jnp.where(key[other] <= key[r], 1, 0)
            elif other > r:
                rank = rank + jnp.where(key[other] < key[r], 1, 0)
        ranks.append(rank)
        hit = lane_dp == own[r]
        asked_row = jnp.where(
            hit & (seen == lane_place), jnp.where(is_slot, slots[r % 2, r // 2], rank), asked_row
        )
        seen = seen + hit.astype(jnp.int32)
        list_row = jnp.where(lane == rank, 2 * own[r] + before, list_row)
        list_row = jnp.where(lane == rank + n_req, r, list_row)
    my_rows = jnp.concatenate([asked_row, list_row], axis=0)
    b["row"][...] = my_rows

    pl.semaphore_wait(barrier, n_dp - 1 + 3)

    met, met_s = b["met"], b["met_s"]

    def ask(i, carry):
        send_to(
            b["row"], met.at[me], b["meta_send"], b["meta_recv"], lax.rem(me + i, n_dp), t
        ).start()
        return carry

    lax.fori_loop(1, n_dp, ask, 0)
    met[me] = my_rows
    others = met.at[pl.ds(0, n_dp - 1)]
    landed_all(others, b["meta_recv"])
    to_smem = pltpu.make_async_copy(met, met_s, b["load_sem"].at[5])
    loads[0].wait()
    to_smem.start()
    to_smem.wait()

    share = b["share"]

    def y_copy(k, g, i, from_y):
        return send_to(
            b["y_out"][k][g].at[i - 1],
            b["cand"][k][g].at[from_y],
            b["y_send"].at[k, g],
            b["y_recv"].at[k, g],
            z * N_Y + lax.rem(y + i, N_Y),
            t,
        )

    def y_pieces(k, g, to_y):
        lo, w = chunks[k]
        for n, d in enumerate(FWD_GROUPS[g]):
            for c in range(2):
                index = jnp.maximum(met_s[up(d) * N_Y + to_y, 0, c * n_dp + me], 0)
                yield n, c, share[index, :, lo : lo + w]

    def y_build(k, g):
        for i in range(1, N_Y):
            for n, c, piece in y_pieces(k, g, lax.rem(y + i, N_Y)):
                b["y_out"][k][g][i - 1, n, c] = piece
            y_copy(k, g, i, y).start()
        for n, c, piece in y_pieces(k, g, y):
            b["cand"][k][g][y, n, c] = piece

    def ring_copy(k, s, up_way, forward):
        rings, first, ss, rs = (
            (b["ring"], b["first"], b["ring_send"], b["ring_recv"])
            if forward
            else (b["back"], b["lists"], b["back_send"], b["back_recv"])
        )
        from_up = up_way if forward else not up_way
        rows = pl.ds(0 if from_up else side, side)
        src = first[k] if s == 1 else ring_slot(rings, k, s - 1)
        return send_to(
            src.at[rows],
            ring_slot(rings, k, s).at[rows],
            ss.at[k, 0 if up_way else 1],
            rs.at[k, s - 1],
            up(1 if up_way else N_Z - 1) * N_Y + y,
            t,
        )

    def ring_slot(rings, k, s):
        pair, at = {1: (0, 0), 2: (1, 0), 6: (1, 1), 3: (2, 0), 5: (2, 1), 4: (3, 0)}[s]
        return rings[k][pair].at[at]

    def merge(k, buf, dist, fresh):
        for down in range(2):
            d = (N_Z - dist) % N_Z if down else dist
            g, n = find_group(FWD_GROUPS, d)
            cand = b["cand"][k][g]
            asker = up(d)

            def one(j, carry, down=down, cand=cand, asker=asker, n=n):
                slot = down * side + j
                code = met_s[asker * N_Y + y, 1, slot]
                mine = cand[lax.rem(lax.div(code, 2), N_Y), n, lax.rem(code, 2)]
                if not fresh:
                    here = lax.div(code, 2 * N_Y) == z
                    mine = jnp.where(here, mine, buf[slot])
                buf[slot] = mine
                return carry

            lax.fori_loop(0, side, one, 0)

    def share_of(owner_t, row, n):
        return b["nb"].at[pl.ds(row, n), pl.ds(owner_t * ts, ts)]

    def gather_start(c, lo, w):
        own_rows = b["sel"].at[pl.ds(2 * c, 2), :, pl.ds(lo, w)]
        there = b["nb"].at[pl.ds(2 * c, 2), pl.ds(t * ts, ts), pl.ds(lo, w)]
        for to_x in (x_up, x_down):
            send_to(
                own_rows, there, b["gx_send"].at[c], b["gx_recv"].at[c], me, to_x * 2 + core
            ).start()
        send_to(own_rows, there, b["gm_send"].at[c], b["gm_recv"].at[c], me, mate).start()

    def gather_pass(c):
        landed_all(b["nb"].at[pl.ds(2 * c, 2), pl.ds(0, 2 * ts)], b["gx_recv"].at[c])
        for from_x, to_x, way in ((x_down, x_up, 0), (x_up, x_down, 1)):
            one = share_of(from_x * 2 + core, 2 * c + way, 1)
            send_to(
                one, one, b["gf_send"].at[c], b["gf_recv"].at[c], me, to_x * 2 + core
            ).start()
        for from_x in (x_down, x_up):
            near = share_of(from_x * 2 + core, 2 * c, 2)
            send_to(near, near, b["gm_send"].at[c], b["gm_recv"].at[c], me, mate).start()

    def gather_far(c):
        far_share = share_of(x_far * 2 + core, 2 * c, 2)
        landed_all(far_share, b["gf_recv"].at[c])
        send_to(far_share, far_share, b["gm_send"].at[c], b["gm_recv"].at[c], me, mate).start()

    def gather_arrived(c):
        landed_all(
            b["nb"].at[pl.ds(2 * c, 2), pl.ds(0, N_X * ts)], b["gm_recv"].at[c]
        )

    def gather_sent(c):
        landed_all(b["nb"].at[pl.ds(2 * c, 2), pl.ds(0, 2 * ts)], b["gx_send"].at[c])
        landed_all(b["sel"].at[pl.ds(2 * c, 2)], b["gf_send"].at[c])
        landed_all(b["nb"].at[pl.ds(2 * c, 2), pl.ds(0, N_X * ts)], b["gm_send"].at[c])

    order = ring_order(chunks, HOPS + 1, False)
    needs = []
    for s, k in order:
        for d in (HOPS + 1 - s, (N_Z - HOPS - 1 + s) % N_Z):
            pair = (k, find_group(FWD_GROUPS, d)[0])
            if pair not in needs:
                needs.append(pair)
    built, landed = 0, []
    for at, (s, k) in enumerate(order):
        dist = HOPS + 1 - s
        wanted = []
        for s2, k2 in order[at : at + 1 + AHEAD]:
            wanted.append((k2, find_group(FWD_GROUPS, HOPS + 1 - s2)[0]))
        while any(pair in needs[built:] for pair in wanted):
            y_build(*needs[built])
            built += 1
        if s > 1:
            landed_all(ring_slot(b["ring"], k, s - 1), b["ring_recv"].at[k, s - 2])
        g = find_group(FWD_GROUPS, dist)[0]
        if (k, g) not in landed:
            landed_all(b["cand"][k][g].at[pl.ds(0, N_Y - 1)], b["y_recv"].at[k, g])
            landed.append((k, g))
        buf = b["first"][k] if s == 1 else ring_slot(b["ring"], k, s - 1)
        merge(k, buf, dist, s == 1)
        if s <= HOPS:
            for up_way in (True, False):
                if s > 1:
                    ring_copy(k, s - 1, up_way, True).wait_send()
                ring_copy(k, s, up_way, True).start()
            continue
        lo, w = chunks[k]
        for r in range(n_req):
            b["sel"][r, :, lo : lo + w] = buf[ranks[r]]
        for c in range(min(GATHER_AHEAD, spans)):
            gather_start(c, lo, w)
    b["nb"][:, pl.ds(pl.multiple_of(t * ts, ts), ts), :] = b["sel"][...]

    back_order = [d for members in BWD_GROUPS for d in members]
    per = LANES // ts
    lane_tok = lax.rem(lane, ts)
    lane_piece = lax.div(lane, ts)
    tall = lax.broadcasted_iota(jnp.int32, (b["place"].shape[0], LANES), 0)
    for group in range(b["place"].shape[1] // LANES):
        line = jnp.full((1, LANES), -1, jnp.int32)
        for j in range(per):
            piece = group * per + j
            c, pos, from_y = piece % 2, piece // 2 % N_Z, piece // 2 // N_Z
            slab = met_s[up(back_order[pos]) * N_Y + from_y, 0, c * n_dp + me]
            line = jnp.where(lane_piece == j, slab * ts + lane_tok, line)
        b["place"][:, group * LANES : (group + 1) * LANES] = jnp.where(
            tall == line, 1.0, 0.0
        ).astype(bf16)

    for load in loads[1:]:
        load.wait()
    for c in range(min(PASS_AHEAD, spans)):
        gather_pass(c)
    for c in range(min(FAR_AHEAD, spans)):
        gather_far(c)

    def mate_copy(c):
        rows = pl.ds(2 * c, 2)
        return send_to(
            b["dn"].at[1 - core, :, rows],
            b["from_mate"].at[:, rows],
            b["rm_send"].at[c],
            b["rm_recv"].at[c],
            me,
            mate,
        )

    def rows_to(to_x, src, dst, ss, rs):
        return send_to(src, dst, ss, rs, me, to_x * 2 + core)

    def far_copy(c, way):
        row = pl.ds(2 * c + way, 1)
        return rows_to(
            x_down if way else x_up,
            b["chip"].at[x_far, row],
            b["from_far"].at[way, pl.ds(c, 1)],
            b["rf_send"].at[c],
            b["rf_recv"].at[c],
        )

    def near_copy(c, way):
        rows = pl.ds(2 * c, 2)
        to_x = x_down if way else x_up
        return rows_to(
            to_x,
            b["chip"].at[to_x, rows],
            b["from_near"].at[way, rows],
            b["rn_send"].at[c],
            b["rn_recv"].at[c],
        )

    def pair_sum(c):
        mate_copy(c).wait_recv()
        rows = pl.ds(2 * c, 2)
        both = b["dn"][core, :, rows].astype(jnp.float32) + b["from_mate"][:, rows].astype(jnp.float32)
        b["chip"][:, rows] = both.astype(bf16)
        for way in range(2):
            far_copy(c, way).start()

    def near_sum(c):
        landed_all(b["from_far"].at[:, pl.ds(c, 1)], b["rf_recv"].at[c])
        for way in range(2):
            to_x, row = x_down if way else x_up, 2 * c + way
            both = b["chip"][to_x, row].astype(jnp.float32) + b["from_far"][way, c].astype(jnp.float32)
            b["chip"][to_x, row] = both.astype(bf16)
            near_copy(c, way).start()

    def last_sum(c):
        rows = pl.ds(2 * c, 2)
        total = b["chip"][x, rows].astype(jnp.float32)
        landed_all(b["from_near"].at[:, rows], b["rn_recv"].at[c])
        for way in range(2):
            total = total + b["from_near"][way, rows].astype(jnp.float32)
        b["total"][rows] = total.astype(bf16)

    def span(c, carry):
        @pl.when(c + GATHER_AHEAD < spans)
        def _():
            gather_start(c + GATHER_AHEAD, 0, enc)

        @pl.when(c + PASS_AHEAD < spans)
        def _():
            gather_pass(c + PASS_AHEAD)

        @pl.when(c + FAR_AHEAD < spans)
        def _():
            gather_far(c + FAR_AHEAD)

        gather_arrived(c)
        tokens = pl.ds(pl.multiple_of(c * SPAN, SPAN), SPAN)
        rows = b["nb"][pl.ds(2 * c, 2)].reshape(2 * n_tokens, enc)
        att_c, dq_c, dn_c = span_grads(
            b["q"][tokens, :], b["g"][tokens, :], rows, b["wk"][...], b["wv"][...]
        )
        b["att_v"][tokens, :] = att_c
        b["dq_v"][tokens, :] = dq_c
        for rr in range(2):
            for to_t in range(n_tp):
                lo = rr * n_tokens + to_t * ts
                b["dn"][to_t % 2, to_t // 2, 2 * c + rr] = dn_c[lo : lo + ts]
        mate_copy(c).start()

        @pl.when(c >= 1)
        def _():
            pair_sum(c - 1)

        @pl.when(c >= 2)
        def _():
            near_sum(c - 2)

        @pl.when(c >= 3)
        def _():
            last_sum(c - 3)

        return carry

    lax.fori_loop(0, spans, span, 0)
    stores = [
        pltpu.make_async_copy(b["att_v"], att, b["load_sem"].at[6]),
        pltpu.make_async_copy(b["dq_v"], dq, b["load_sem"].at[7]),
    ]
    for store in stores:
        store.start()
    pair_sum(spans - 1)
    for c in range(max(spans - 2, 0), spans):
        near_sum(c)
    for c in range(max(spans - 3, 0), spans):
        last_sum(c)

    def yb_copy(k, h, i, from_y):
        at = sum(len(m) for m in BWD_GROUPS[:h])
        return send_to(
            b["yb_out"][k][h].at[i - 1],
            b["got"][k].at[from_y, pl.ds(at, len(BWD_GROUPS[h]))],
            b["yb_send"].at[k, h],
            b["yb_recv"].at[k, h],
            z * N_Y + lax.rem(y + i, N_Y),
            t,
        )

    def yb_pieces(k, h, to_y):
        for n, d in enumerate(BWD_GROUPS[h]):
            for c in range(2):
                j = met_s[up(d) * N_Y + y, 0, (2 + c) * n_dp + z * N_Y + to_y]
                j = jnp.minimum(jnp.maximum(j, 0), n_req - 1)
                if d == 0:
                    piece = b["lists"][k][j]
                elif d in (1, 7, 4):
                    piece = b["back"][k][0 if d != 4 else 3][0, j]
                else:
                    early = jnp.where(j < side, d, N_Z - d) < 4
                    piece = b["back"][k][1 if d in (2, 6) else 2][jnp.where(early, 0, 1), j]
                yield n, c, piece

    def yb_build(k, h):
        at = sum(len(m) for m in BWD_GROUPS[:h])
        for i in range(1, N_Y):
            for n, c, piece in yb_pieces(k, h, lax.rem(y + i, N_Y)):
                b["yb_out"][k][h][i - 1, n, c] = piece
            yb_copy(k, h, i, y).start()
        for n, c, piece in yb_pieces(k, h, y):
            b["got"][k][y, at + n, c] = piece

    for s, k in ring_order(chunks, HOPS + 1, True):
        if s == 1:
            lo, w = chunks[k]
            for j in range(n_req):
                b["lists"][k][j] = b["total"][met_s[me, 1, n_req + j], :, lo : lo + w]
        if s > 1:
            landed_all(ring_slot(b["back"], k, s - 1), b["back_recv"].at[k, s - 2])
        if s <= HOPS:
            for up_way in (True, False):
                if s > 1:
                    ring_copy(k, s - 1, up_way, False).wait_send()
                ring_copy(k, s, up_way, False).start()
        if s - 1 in BWD_READY:
            yb_build(k, BWD_READY[s - 1])

    for k, (lo, w) in enumerate(chunks):
        at = 0
        for h, members in enumerate(BWD_GROUPS):
            landed_all(
                b["got"][k].at[pl.ds(0, N_Y - 1), pl.ds(at, len(members))], b["yb_recv"].at[k, h]
            )
            at += len(members)
        pieces = b["got"][k][...].reshape(b["place"].shape[1], w)
        dt[:, :, lo : lo + w] = nn(b["place"][...], pieces).reshape(dt.shape[0], ts, w)

    for store in stores:
        store.wait()
    landed_all(others, b["meta_send"])
    for k in range(nk):
        for g in range(len(FWD_GROUPS)):
            landed_all(b["y_out"][k][g], b["y_send"].at[k, g])
            landed_all(b["yb_out"][k][g], b["yb_send"].at[k, g])
        for up_way in (True, False):
            ring_copy(k, HOPS, up_way, True).wait_send()
            ring_copy(k, HOPS, up_way, False).wait_send()

    def drain(c, carry):
        gather_sent(c)
        mate_copy(c).wait_send()
        landed_all(b["from_far"].at[:, pl.ds(c, 1)], b["rf_send"].at[c])
        landed_all(b["from_near"].at[:, pl.ds(2 * c, 2)], b["rn_send"].at[c])
        return carry

    lax.fori_loop(0, spans, drain, 0)


def finish_kernel(att_in, dq_in, dt_in, att, dq, dt):
    att[...] = att_in[...]
    dq[...] = dq_in[...]
    dt[...] = dt_in[...]


def finish(*arrays):
    parts = 4

    def spec(a):
        block = (a.shape[0] // parts, *a.shape[1:])
        return pl.BlockSpec(block, lambda i: (i,) + (0,) * (len(block) - 1))

    return pl.pallas_call(
        finish_kernel,
        grid=(parts,),
        out_shape=[jax.ShapeDtypeStruct(a.shape, a.dtype) for a in arrays],
        in_specs=[spec(a) for a in arrays],
        out_specs=[spec(a) for a in arrays],
        name="finish",
    )(*arrays)


def on_device(queries, cotangent, table, key_weight, value_weight, owners, slots):
    n_dp = lax.axis_size("dp")
    n_tp = lax.axis_size("tensor")
    n_slabs, n_tokens, enc = table.shape
    ts = n_tokens // n_tp
    spans = owners.shape[0]
    n_req = 2 * spans
    n_x = n_tp // 2
    chunks = lane_chunks(enc)
    nk = len(chunks)
    dma = pltpu.SemaphoreType.DMA
    bf16 = jnp.bfloat16
    vm = lambda *shape: pltpu.VMEM(shape, bf16)
    ng = len(FWD_GROUPS)
    rings = lambda w: [vm(n, n_req, ts, w) for n in (1, 2, 2, 1)]
    scratch = dict(
        share=vm(n_slabs, ts, enc),
        wk=vm(*key_weight.shape),
        wv=vm(*value_weight.shape),
        q=vm(*queries.shape),
        g=vm(*cotangent.shape),
        att_v=vm(*queries.shape),
        dq_v=vm(*queries.shape),
        row=pltpu.VMEM((2, LANES), jnp.int32),
        met=pltpu.VMEM((n_dp, 2, LANES), jnp.int32),
        met_s=pltpu.SMEM((n_dp, 2, LANES), jnp.int32),
        y_out=[[vm(N_Y - 1, len(m), 2, ts, w) for m in FWD_GROUPS] for _, w in chunks],
        cand=[[vm(N_Y, len(m), 2, ts, w) for m in FWD_GROUPS] for _, w in chunks],
        first=[vm(n_req, ts, w) for _, w in chunks],
        ring=[rings(w) for _, w in chunks],
        sel=vm(n_req, ts, enc),
        nb=vm(n_req, n_tokens, enc),
        place=vm(n_slabs * ts, 2 * n_dp * ts),
        dn=vm(2, n_x, n_req, ts, enc),
        from_mate=vm(n_x, n_req, ts, enc),
        chip=vm(n_x, n_req, ts, enc),
        from_far=vm(2, spans, ts, enc),
        from_near=vm(2, n_req, ts, enc),
        total=vm(n_req, ts, enc),
        lists=[vm(n_req, ts, w) for _, w in chunks],
        back=[rings(w) for _, w in chunks],
        yb_out=[[vm(N_Y - 1, len(m), 2, ts, w) for m in BWD_GROUPS] for _, w in chunks],
        got=[vm(N_Y, N_Z, 2, ts, w) for _, w in chunks],
        load_sem=dma((8,)),
        meta_send=dma,
        meta_recv=dma,
        y_send=dma((nk, ng)),
        y_recv=dma((nk, ng)),
        yb_send=dma((nk, ng)),
        yb_recv=dma((nk, ng)),
        ring_send=dma((nk, 2)),
        ring_recv=dma((nk, HOPS)),
        back_send=dma((nk, 2)),
        back_recv=dma((nk, HOPS)),
        gx_send=dma((spans,)),
        gx_recv=dma((spans,)),
        gf_send=dma((spans,)),
        gf_recv=dma((spans,)),
        gm_send=dma((spans,)),
        gm_recv=dma((spans,)),
        rm_send=dma((spans,)),
        rm_recv=dma((spans,)),
        rf_send=dma((spans,)),
        rf_recv=dma((spans,)),
        rn_send=dma((spans,)),
        rn_recv=dma((spans,)),
    )
    leaves, treedef = jax.tree_util.tree_flatten(scratch)
    anywhere = pl.BlockSpec(memory_space=pl.ANY)
    results = pl.pallas_call(
        functools.partial(fused_kernel, n_dp, n_tp, treedef),
        out_shape=[
            jax.ShapeDtypeStruct(queries.shape, bf16),
            jax.ShapeDtypeStruct(queries.shape, bf16),
            jax.ShapeDtypeStruct((n_slabs, ts, enc), jnp.float32),
        ],
        in_specs=[pl.BlockSpec(memory_space=pltpu.SMEM)] * 2 + [anywhere] * 5,
        out_specs=[anywhere, anywhere, pl.BlockSpec(memory_space=pltpu.VMEM)],
        scratch_shapes=leaves,
        compiler_params=pltpu.CompilerParams(
            collective_id=0, has_side_effects=True, vmem_limit_bytes=VMEM_LIMIT
        ),
        name="spanned",
    )(owners.T, slots.T, table, queries, cotangent, key_weight, value_weight)
    return finish(*results)


def solution(mesh):
    in_specs = (
        P("dp", "tensor"),
        P("dp", "tensor"),
        P("dp", None, None),
        P(None, "tensor"),
        P(None, "tensor"),
        P("dp", None),
        P("dp", None),
    )
    out_specs = (P("dp", "tensor"), P("dp", "tensor"), P("dp", "tensor", None))
    return jax.shard_map(
        on_device, mesh=mesh, in_specs=in_specs, out_specs=out_specs, check_vma=False
    )
```

```python
import functools
import math
import types

import jax
import jax.numpy as jnp
from jax import lax
from jax.experimental import pallas as pl
from jax.experimental.pallas import tpu as pltpu
from jax.sharding import PartitionSpec as P

HD = 128
SPAN = 64
LANES = 128
N_Y = 4
N_Z = 8
HOPS = 4
N_X = 4
FAR_SLOTS = 4
WAVES = 2
CHUNKS = 3
AHEAD = 4
FWD_GROUPS = ((4,), (3, 5), (2, 6), (1, 7, 0))
BWD_GROUPS = ((0, 1, 7), (2, 6), (3, 5), (4,))
MESH = pl.DeviceIdType.MESH
VMEM_LIMIT = 56 * 1024 * 1024


def lane_chunks(enc):
    units = enc // LANES
    count = min(CHUNKS, units)
    chunks = []
    at = 0
    for left in range(count, 0, -1):
        n = (units - at) // left
        chunks.append((at * LANES, n * LANES))
        at += n
    return chunks


def find_group(groups, d):
    for g, members in enumerate(groups):
        if d in members:
            return g, members.index(d)


def nt(a, b):
    return lax.dot_general(a, b, (((1,), (1,)), ((), ())), preferred_element_type=jnp.float32)


def tn(a, b):
    return lax.dot_general(a, b, (((0,), (0,)), ((), ())), preferred_element_type=jnp.float32)


def nn(a, b):
    return lax.dot_general(a, b, (((1,), (0,)), ((), ())), preferred_element_type=jnp.float32)


def span_grads(q, g, rows, wk, wv):
    bf16 = jnp.bfloat16
    scale = 1.0 / math.sqrt(HD)
    heads = q.shape[1] // HD
    keys = nn(rows, wk).astype(bf16)
    values = nn(rows, wv).astype(bf16)
    cut = [slice(h * HD, (h + 1) * HD) for h in range(heads)]
    scores = jnp.concatenate([nt(q[:, s], keys[:, s]) for s in cut], axis=0) * scale
    d_weights = jnp.concatenate([nt(g[:, s], values[:, s]) for s in cut], axis=0)
    e = jnp.exp(scores - jnp.max(scores, axis=1, keepdims=True))
    probs = e / jnp.sum(e, axis=1, keepdims=True)
    row_sums = jnp.sum(d_weights * probs, axis=1, keepdims=True)
    ds = (probs * (d_weights - row_sums) * scale).astype(bf16)
    weights = probs.astype(bf16)
    attended, d_query, d_keys, d_values = [], [], [], []
    for h, s in enumerate(cut):
        w_h = weights[h * SPAN : (h + 1) * SPAN]
        ds_h = ds[h * SPAN : (h + 1) * SPAN]
        attended.append(nn(w_h, values[:, s]).astype(bf16))
        d_query.append(nn(ds_h, keys[:, s]).astype(bf16))
        d_keys.append(tn(ds_h, q[:, s]).astype(bf16))
        d_values.append(tn(w_h, g[:, s]).astype(bf16))
    dn = nt(jnp.concatenate(d_keys, axis=1), wk) + nt(jnp.concatenate(d_values, axis=1), wv)
    return (
        jnp.concatenate(attended, axis=1),
        jnp.concatenate(d_query, axis=1),
        dn.astype(bf16),
    )


def fused_kernel(
    n_dp, n_tp, treedef, owners, slots, table, queries, cotangent, key_weight, value_weight, att, dq, dt, *flat
):
    b = types.SimpleNamespace(**jax.tree_util.tree_unflatten(treedef, flat))
    bf16 = jnp.bfloat16
    me = lax.axis_index("dp")
    t = lax.axis_index("tensor")
    z, y = lax.div(me, N_Y), lax.rem(me, N_Y)
    x, core = lax.div(t, 2), lax.rem(t, 2)
    mate = x * 2 + 1 - core
    x_up, x_far, x_down = [lax.rem(x + i, N_X) for i in range(1, N_X)]
    n_req, ts, enc = b.sel.shape
    spans = n_req // 2
    wave_spans = spans // WAVES
    side = n_req // WAVES
    n_tokens = ts * n_tp
    chunks = lane_chunks(enc)
    nk = len(chunks)

    def up(d):
        return lax.rem(z + d, N_Z)

    def send_to(src, dst, ss, rs, dp_to, t_to):
        return pltpu.make_async_remote_copy(
            src_ref=src, dst_ref=dst, send_sem=ss, recv_sem=rs, device_id=(dp_to, t_to), device_id_type=MESH
        )

    def landed_all(ref, sem):
        pltpu.make_async_copy(ref, ref, sem).wait()

    loads = [
        pltpu.make_async_copy(table.at[:, pl.ds(t * ts, ts), :], b.share, b.load_sem.at[0]),
        pltpu.make_async_copy(key_weight, b.wk, b.load_sem.at[1]),
        pltpu.make_async_copy(value_weight, b.wv, b.load_sem.at[2]),
        pltpu.make_async_copy(queries, b.q, b.load_sem.at[3]),
        pltpu.make_async_copy(cotangent, b.g, b.load_sem.at[4]),
    ]
    for load in loads:
        load.start()

    barrier = pltpu.get_barrier_semaphore()
    def hello(i, carry):
        pl.semaphore_signal(
            barrier, inc=1, device_id=(lax.rem(me + i, n_dp), t), device_id_type=MESH
        )
        return carry

    lax.fori_loop(1, n_dp, hello, 0)
    for peer_t in (x_up * 2 + core, x_down * 2 + core, mate):
        pl.semaphore_signal(barrier, inc=1, device_id=(me, peer_t), device_id_type=MESH)

    lane = lax.broadcasted_iota(jnp.int32, (1, LANES), 1)
    lane_dp = lane & (n_dp - 1)
    lane_place = lax.shift_right_logical(lane, int(math.log2(n_dp))) & 1
    is_slot = lane < 2 * n_dp
    own = [owners[r % 2, r // 2] for r in range(n_req)]
    far = [lax.rem(z - lax.div(own[r], N_Y) + N_Z, N_Z) for r in range(n_req)]
    asked_row = jnp.full((1, LANES), -1, jnp.int32)
    list_row = jnp.zeros((1, LANES), jnp.int32)
    seen = jnp.zeros((1, LANES), jnp.int32)
    ranks = []
    for wave in range(WAVES):
        members = range(wave * side, (wave + 1) * side)
        taken = jnp.int32(0)
        down, dist = {}, {}
        for r in members:
            opposite = jnp.where(far[r] == HOPS, 1, 0)
            over = opposite * jnp.where(taken >= FAR_SLOTS, 1, 0)
            down[r] = jnp.where(far[r] > HOPS, 1, over)
            dist[r] = jnp.where(down[r] == 1, N_Z - far[r], far[r])
            taken = taken + opposite
        for r in members:
            slot = down[r] * side
            before = jnp.int32(0)
            for other in range(r):
                before = before + jnp.where(own[other] == own[r], 1, 0)
            for other in members:
                if other != r:
                    ahead = (dist[other] >= dist[r]) if other < r else (dist[other] > dist[r])
                    slot = slot + jnp.where(down[other] == down[r], 1, 0) * jnp.where(ahead, 1, 0)
            ranks.append(slot)
            hit = lane_dp == own[r]
            asked_row = jnp.where(
                hit & (seen == lane_place),
                jnp.where(is_slot, slots[r % 2, r // 2], wave * 2 * side + slot),
                asked_row,
            )
            seen = seen + hit.astype(jnp.int32)
            list_row = jnp.where(lane == wave * 2 * side + slot, 2 * own[r] + before, list_row)
            list_row = jnp.where(lane == (WAVES + wave) * 2 * side + slot, r, list_row)
    my_rows = jnp.concatenate([asked_row, list_row], axis=0)
    b.row[...] = my_rows

    pl.semaphore_wait(barrier, n_dp - 1 + 3)

    met, met_s = b.met, b.met_s

    def ask(i, carry):
        send_to(
            b.row, met.at[me], b.meta_send, b.meta_recv, lax.rem(me + i, n_dp), t
        ).start()
        return carry

    lax.fori_loop(1, n_dp, ask, 0)
    met[me] = my_rows
    others = met.at[pl.ds(0, n_dp - 1)]
    landed_all(others, b.meta_recv)
    to_smem = pltpu.make_async_copy(met, met_s, b.load_sem.at[5])
    loads[0].wait()
    to_smem.start()
    to_smem.wait()

    share = b.share

    def y_copy(k, g, i, from_y):
        return send_to(
            b.y_out[k][g].at[i - 1],
            b.cand[k][g].at[from_y],
            b.y_send.at[k, g],
            b.y_recv.at[k, g],
            z * N_Y + lax.rem(y + i, N_Y),
            t,
        )

    def y_pieces(k, g, to_y):
        lo, w = chunks[k]
        for n, d in enumerate(FWD_GROUPS[g]):
            for c in range(2):
                index = jnp.maximum(met_s[up(d) * N_Y + to_y, 0, c * n_dp + me], 0)
                yield n, c, share[index, :, lo : lo + w]

    def y_build(k, g):
        for i in range(1, N_Y):
            for n, c, piece in y_pieces(k, g, lax.rem(y + i, N_Y)):
                b.y_out[k][g][i - 1, n, c] = piece
            y_copy(k, g, i, y).start()
        for n, c, piece in y_pieces(k, g, y):
            b.cand[k][g][y, n, c] = piece

    def ring_rows(s, lower, forward):
        hop = HOPS + 1 - s if forward else s
        return pl.ds(0 if lower else side, FAR_SLOTS if hop == HOPS else side)

    def ring_slot(forward, wave, k, s):
        if forward:
            return b.first[wave][k] if s == 0 else b.ring[wave][k][s - 1]
        return b.lists[k].at[wave] if s == 0 else b.back[k][s - 1].at[wave]

    def ring_copy(forward, wave, k, s, up_way):
        ss, rs = (
            (b.ring_send, b.ring_recv) if forward else (b.back_send, b.back_recv)
        )
        rows = ring_rows(s, up_way if forward else not up_way, forward)
        return send_to(
            ring_slot(forward, wave, k, s - 1).at[rows],
            ring_slot(forward, wave, k, s).at[rows],
            ss.at[wave, k, 0 if up_way else 1],
            rs.at[wave, k, s - 1],
            up(1 if up_way else N_Z - 1) * N_Y + y,
            t,
        )

    def ring_step(forward, wave, k, s):
        for up_way in (True, False):
            if s > 1:
                ring_copy(forward, wave, k, s - 1, up_way).wait_send()
            ring_copy(forward, wave, k, s, up_way).start()

    def ring_landed(forward, wave, k, s):
        rs = b.ring_recv if forward else b.back_recv
        hop = HOPS + 1 - s if forward else s
        rows = pl.ds(0, 2 * (FAR_SLOTS if hop == HOPS else side))
        landed_all(ring_slot(forward, wave, k, s).at[rows], rs.at[wave, k, s - 1])

    def merge(wave, k, buf, dist):
        for down in range(2):
            d = (N_Z - dist) % N_Z if down else dist
            g, n = find_group(FWD_GROUPS, d)
            cand = b.cand[k][g]
            asker = up(d) * N_Y + y

            def one(j, carry, fresh, down=down, cand=cand, asker=asker, n=n):
                slot = down * side + j
                code = met_s[asker, 1, wave * 2 * side + slot]
                mine = cand[lax.shift_right_logical(code, 1) & (N_Y - 1), n, code & 1]
                if not fresh:
                    here = lax.div(code, 2 * N_Y) == z
                    mine = jnp.where(here, mine, buf[slot])
                buf[slot] = mine
                return carry

            if dist == HOPS:
                lax.fori_loop(0, FAR_SLOTS, functools.partial(one, fresh=True), 0)
            elif dist == HOPS - 1:
                lax.fori_loop(0, FAR_SLOTS, functools.partial(one, fresh=False), 0)
                lax.fori_loop(FAR_SLOTS, side, functools.partial(one, fresh=True), 0)
            else:
                lax.fori_loop(0, side, functools.partial(one, fresh=False), 0)

    def share_of(owner_t, row, n):
        return b.nb.at[pl.ds(row, n), pl.ds(owner_t * ts, ts)]

    def gather_start(c, lo, w):
        own_rows = b.sel.at[pl.ds(2 * c, 2), :, pl.ds(lo, w)]
        there = b.nb.at[pl.ds(2 * c, 2), pl.ds(t * ts, ts), pl.ds(lo, w)]
        for to_x in (x_up, x_down):
            send_to(
                own_rows, there, b.gx_send.at[c], b.gx_recv.at[c], me, to_x * 2 + core
            ).start()
        send_to(own_rows, there, b.gm_send.at[c], b.gm_recv.at[c], me, mate).start()

    def gather_pass(c):
        landed_all(b.nb.at[pl.ds(2 * c, 2), pl.ds(0, 2 * ts)], b.gx_recv.at[c])
        for from_x, to_x, way in ((x_down, x_up, 0), (x_up, x_down, 1)):
            one = share_of(from_x * 2 + core, 2 * c + way, 1)
            send_to(
                one, one, b.gf_send.at[c], b.gf_recv.at[c], me, to_x * 2 + core
            ).start()
        for from_x in (x_down, x_up):
            near = share_of(from_x * 2 + core, 2 * c, 2)
            send_to(near, near, b.gm_send.at[c], b.gm_recv.at[c], me, mate).start()

    def gather_far(c):
        far_share = share_of(x_far * 2 + core, 2 * c, 2)
        landed_all(far_share, b.gf_recv.at[c])
        send_to(far_share, far_share, b.gm_send.at[c], b.gm_recv.at[c], me, mate).start()

    def gather_arrived(c):
        landed_all(
            b.nb.at[pl.ds(2 * c, 2), pl.ds(0, N_X * ts)], b.gm_recv.at[c]
        )

    def gather_sent(c):
        landed_all(b.nb.at[pl.ds(2 * c, 2), pl.ds(0, 2 * ts)], b.gx_send.at[c])
        landed_all(b.sel.at[pl.ds(2 * c, 2)], b.gf_send.at[c])
        landed_all(b.nb.at[pl.ds(2 * c, 2), pl.ds(0, N_X * ts)], b.gm_send.at[c])

    needs = [(k, g) for g in range(len(FWD_GROUPS)) for k in range(nk)]
    built, landed = [0], []

    def fetch_step(wave, k, s):
        dist = HOPS + 1 - s
        g = find_group(FWD_GROUPS, dist)[0]
        while built[0] < len(needs) and built[0] <= needs.index((k, g)) + AHEAD:
            y_build(*needs[built[0]])
            built[0] += 1
        if s > 1:
            ring_landed(True, wave, k, s - 1)
        if (k, g) not in landed:
            landed_all(b.cand[k][g].at[pl.ds(0, N_Y - 1)], b.y_recv.at[k, g])
            landed.append((k, g))
        buf = ring_slot(True, wave, k, s - 1)
        merge(wave, k, buf, dist)
        if s <= HOPS:
            ring_step(True, wave, k, s)
            return
        lo, w = chunks[k]
        for r in range(wave * side, (wave + 1) * side):
            b.sel[r, :, lo : lo + w] = buf[ranks[r]]
        for c in range(wave * wave_spans, (wave + 1) * wave_spans):
            gather_start(c, lo, w)
        if k == nk - 1:
            rows = pl.ds(wave * side, side)
            b.nb[rows, pl.ds(pl.multiple_of(t * ts, ts), ts), :] = b.sel[rows]

    back_order = [d for members in BWD_GROUPS for d in members]

    def build_place():
        per = LANES // ts
        lane_tok = lax.rem(lane, ts)
        lane_piece = lax.div(lane, ts)
        tall = lax.broadcasted_iota(jnp.int32, (b.place.shape[0], LANES), 0)
        for group in range(b.place.shape[1] // LANES):
            line = jnp.full((1, LANES), -1, jnp.int32)
            for j in range(per):
                piece = group * per + j
                c, pos, from_y = piece % 2, piece // 2 % N_Z, piece // 2 // N_Z
                slab = met_s[up(back_order[pos]) * N_Y + from_y, 0, c * n_dp + me]
                line = jnp.where(lane_piece == j, slab * ts + lane_tok, line)
            b.place[:, group * LANES : (group + 1) * LANES] = jnp.where(
                tall == line, 1.0, 0.0
            ).astype(bf16)

    def mate_copy(c):
        rows = pl.ds(2 * c, 2)
        return send_to(
            b.dn.at[1 - core, :, rows],
            b.from_mate.at[:, rows],
            b.rm_send.at[c],
            b.rm_recv.at[c],
            me,
            mate,
        )

    def rows_to(to_x, src, dst, ss, rs):
        return send_to(src, dst, ss, rs, me, to_x * 2 + core)

    def far_copy(c, way):
        row = pl.ds(2 * c + way, 1)
        return rows_to(
            x_down if way else x_up,
            b.chip.at[x_far, row],
            b.from_far.at[way, pl.ds(c, 1)],
            b.rf_send.at[c],
            b.rf_recv.at[c],
        )

    def near_copy(c, way):
        rows = pl.ds(2 * c, 2)
        to_x = x_down if way else x_up
        return rows_to(
            to_x,
            b.chip.at[to_x, rows],
            b.from_near.at[way, rows],
            b.rn_send.at[c],
            b.rn_recv.at[c],
        )

    def pair_sum(c):
        mate_copy(c).wait_recv()
        rows = pl.ds(2 * c, 2)
        both = b.dn[core, :, rows].astype(jnp.float32) + b.from_mate[:, rows].astype(jnp.float32)
        b.chip[:, rows] = both.astype(bf16)
        for way in range(2):
            far_copy(c, way).start()

    def near_sum(c):
        landed_all(b.from_far.at[:, pl.ds(c, 1)], b.rf_recv.at[c])
        for way in range(2):
            to_x, row = x_down if way else x_up, 2 * c + way
            both = b.chip[to_x, row].astype(jnp.float32) + b.from_far[way, c].astype(jnp.float32)
            b.chip[to_x, row] = both.astype(bf16)
            near_copy(c, way).start()

    def last_sum(c):
        rows = pl.ds(2 * c, 2)
        total = b.chip[x, rows].astype(jnp.float32)
        landed_all(b.from_near.at[:, rows], b.rn_recv.at[c])
        for way in range(2):
            total = total + b.from_near[way, rows].astype(jnp.float32)
        wave = c // wave_spans
        b.total[wave][pl.ds(2 * c - wave * side, 2)] = total.astype(bf16)

    def attend(c):
        gather_arrived(c)
        tokens = pl.ds(c * SPAN, SPAN)
        rows = b.nb[pl.ds(2 * c, 2)].reshape(2 * n_tokens, enc)
        att_c, dq_c, dn_c = span_grads(
            b.q[tokens, :], b.g[tokens, :], rows, b.wk[...], b.wv[...]
        )
        b.att_v[tokens, :] = att_c
        b.dq_v[tokens, :] = dq_c
        for rr in range(2):
            for to_t in range(n_tp):
                lo = rr * n_tokens + to_t * ts
                b.dn[to_t % 2, to_t // 2, 2 * c + rr] = dn_c[lo : lo + ts]
        mate_copy(c).start()

    def back_lists(wave):
        for k, (lo, w) in enumerate(chunks):
            for j in range(2 * side):
                r = met_s[me, 1, (WAVES + wave) * 2 * side + j]
                b.lists[k][wave, j] = b.total[wave][jnp.maximum(r - wave * side, 0), :, lo : lo + w]

    def back_step(wave, k, s):
        if s > 1:
            ring_landed(False, wave, k, s - 1)
        if s <= HOPS:
            ring_step(False, wave, k, s)
        if wave == WAVES - 1 and s > 1:
            yb_build(k, s - 2)

    def yb_copy(k, h, i, from_y):
        at = sum(len(m) for m in BWD_GROUPS[:h])
        return send_to(
            b.yb_out[k][h].at[i - 1],
            b.got[k].at[from_y, pl.ds(at, len(BWD_GROUPS[h]))],
            b.yb_send.at[k, h],
            b.yb_recv.at[k, h],
            z * N_Y + lax.rem(y + i, N_Y),
            t,
        )

    def yb_pieces(k, h, to_y):
        for n, d in enumerate(BWD_GROUPS[h]):
            for c in range(2):
                j = met_s[up(d) * N_Y + y, 0, (2 + c) * n_dp + z * N_Y + to_y]
                j = jnp.maximum(j, 0)
                wave, slot = lax.div(j, 2 * side), lax.rem(j, 2 * side)
                if d == 0:
                    piece = b.lists[k][wave, slot]
                else:
                    piece = b.back[k][min(d, N_Z - d) - 1][wave, slot]
                yield n, c, piece

    def yb_build(k, h):
        at = sum(len(m) for m in BWD_GROUPS[:h])
        for i in range(1, N_Y):
            for n, c, piece in yb_pieces(k, h, lax.rem(y + i, N_Y)):
                b.yb_out[k][h][i - 1, n, c] = piece
            yb_copy(k, h, i, y).start()
        for n, c, piece in yb_pieces(k, h, y):
            b.got[k][y, at + n, c] = piece

    stores = [
        pltpu.make_async_copy(b.att_v, att, b.load_sem.at[6]),
        pltpu.make_async_copy(b.dq_v, dq, b.load_sem.at[7]),
    ]

    def prepare():
        build_place()
        for load in loads[1:]:
            load.wait()

    def store_all():
        for store in stores:
            store.start()

    def ring_job(step, reverse):
        def job(wave, s):
            for k in reversed(range(nk)) if reverse else range(nk):
                step(wave, k, s)

        return job

    fetch_job, back_job = ring_job(fetch_step, False), ring_job(back_step, True)
    order = (
        (fetch_job, 0, 1),
        (fetch_job, 0, 2),
        (fetch_job, 0, 3),
        (fetch_job, 1, 1),
        (fetch_job, 0, 4),
        (prepare,),
        (fetch_job, 0, 5),
        (fetch_job, 1, 2),
        (gather_pass, 0),
        (fetch_job, 1, 3),
        (gather_far, 0),
        (gather_pass, 1),
        (attend, 0),
        (gather_far, 1),
        (gather_pass, 2),
        (fetch_job, 1, 4),
        (attend, 1),
        (pair_sum, 0),
        (gather_far, 2),
        (gather_pass, 3),
        (attend, 2),
        (pair_sum, 1),
        (near_sum, 0),
        (gather_far, 3),
        (fetch_job, 1, 5),
        (attend, 3),
        (pair_sum, 2),
        (near_sum, 1),
        (last_sum, 0),
        (gather_pass, 4),
        (pair_sum, 3),
        (near_sum, 2),
        (last_sum, 1),
        (gather_far, 4),
        (gather_pass, 5),
        (near_sum, 3),
        (last_sum, 2),
        (attend, 4),
        (last_sum, 3),
        (back_lists, 0),
        (back_job, 0, 1),
        (pair_sum, 4),
        (gather_far, 5),
        (gather_pass, 6),
        (attend, 5),
        (back_job, 0, 2),
        (pair_sum, 5),
        (near_sum, 4),
        (gather_far, 6),
        (gather_pass, 7),
        (attend, 6),
        (back_job, 0, 3),
        (pair_sum, 6),
        (near_sum, 5),
        (last_sum, 4),
        (gather_far, 7),
        (attend, 7),
        (store_all,),
        (back_job, 0, 4),
        (pair_sum, 7),
        (near_sum, 6),
        (last_sum, 5),
        (near_sum, 7),
        (last_sum, 6),
        (last_sum, 7),
        (back_lists, 1),
        (back_job, 1, 1),
        (back_job, 0, 5),
        (back_job, 1, 2),
        (back_job, 1, 3),
        (back_job, 1, 4),
        (back_job, 1, 5),
    )
    for job, *numbers in order:
        job(*numbers)

    for k, (lo, w) in enumerate(chunks):
        at = 0
        for h, members in enumerate(BWD_GROUPS):
            landed_all(
                b.got[k].at[pl.ds(0, N_Y - 1), pl.ds(at, len(members))], b.yb_recv.at[k, h]
            )
            at += len(members)
        pieces = b.got[k][...].reshape(b.place.shape[1], w)
        dt[:, :, lo : lo + w] = nn(b.place[...], pieces).reshape(dt.shape[0], ts, w)

    for store in stores:
        store.wait()
    landed_all(others, b.meta_send)
    for k in range(nk):
        for g in range(len(FWD_GROUPS)):
            landed_all(b.y_out[k][g], b.y_send.at[k, g])
            landed_all(b.yb_out[k][g], b.yb_send.at[k, g])
        for wave in range(WAVES):
            for up_way in (True, False):
                ring_copy(True, wave, k, HOPS, up_way).wait_send()
                ring_copy(False, wave, k, HOPS, up_way).wait_send()

    def drain(c, carry):
        gather_sent(c)
        mate_copy(c).wait_send()
        landed_all(b.from_far.at[:, pl.ds(c, 1)], b.rf_send.at[c])
        landed_all(b.from_near.at[:, pl.ds(2 * c, 2)], b.rn_send.at[c])
        return carry

    lax.fori_loop(0, spans, drain, 0)


def finish_kernel(att_in, dq_in, dt_in, att, dq, dt):
    att[...] = att_in[...]
    dq[...] = dq_in[...]
    dt[...] = dt_in[...]


def finish(*arrays):
    parts = 4

    def spec(a):
        block = (a.shape[0] // parts, *a.shape[1:])
        return pl.BlockSpec(block, lambda i: (i,) + (0,) * (len(block) - 1))

    return pl.pallas_call(
        finish_kernel,
        grid=(parts,),
        out_shape=[jax.ShapeDtypeStruct(a.shape, a.dtype) for a in arrays],
        in_specs=[spec(a) for a in arrays],
        out_specs=[spec(a) for a in arrays],
        name="finish",
    )(*arrays)


def on_device(queries, cotangent, table, key_weight, value_weight, owners, slots):
    n_dp = lax.axis_size("dp")
    n_tp = lax.axis_size("tensor")
    n_slabs, n_tokens, enc = table.shape
    ts = n_tokens // n_tp
    spans = owners.shape[0]
    n_req = 2 * spans
    n_x = n_tp // 2
    chunks = lane_chunks(enc)
    nk = len(chunks)
    dma = pltpu.SemaphoreType.DMA
    bf16 = jnp.bfloat16
    vm = lambda *shape: pltpu.VMEM(shape, bf16)
    ng = len(FWD_GROUPS)
    side = n_req // WAVES
    scratch = dict(
        share=vm(n_slabs, ts, enc),
        wk=vm(*key_weight.shape),
        wv=vm(*value_weight.shape),
        q=vm(*queries.shape),
        g=vm(*cotangent.shape),
        att_v=vm(*queries.shape),
        dq_v=vm(*queries.shape),
        row=pltpu.VMEM((2, LANES), jnp.int32),
        met=pltpu.VMEM((n_dp, 2, LANES), jnp.int32),
        met_s=pltpu.SMEM((n_dp, 2, LANES), jnp.int32),
        y_out=[[vm(N_Y - 1, len(m), 2, ts, w) for m in FWD_GROUPS] for _, w in chunks],
        cand=[[vm(N_Y, len(m), 2, ts, w) for m in FWD_GROUPS] for _, w in chunks],
        first=[[vm(2 * side, ts, w) for _, w in chunks] for _ in range(WAVES)],
        ring=[
            [[vm(2 * side, ts, w) for _ in range(HOPS)] for _, w in chunks] for _ in range(WAVES)
        ],
        sel=vm(n_req, ts, enc),
        nb=vm(n_req, n_tokens, enc),
        place=vm(n_slabs * ts, 2 * n_dp * ts),
        dn=vm(2, n_x, n_req, ts, enc),
        from_mate=vm(n_x, n_req, ts, enc),
        chip=vm(n_x, n_req, ts, enc),
        from_far=vm(2, spans, ts, enc),
        from_near=vm(2, n_req, ts, enc),
        total=[vm(side, ts, enc) for _ in range(WAVES)],
        lists=[vm(WAVES, 2 * side, ts, w) for _, w in chunks],
        back=[[vm(WAVES, 2 * side, ts, w) for _ in range(HOPS)] for _, w in chunks],
        yb_out=[[vm(N_Y - 1, len(m), 2, ts, w) for m in BWD_GROUPS] for _, w in chunks],
        got=[vm(N_Y, N_Z, 2, ts, w) for _, w in chunks],
        load_sem=dma((8,)),
        meta_send=dma,
        meta_recv=dma,
        y_send=dma((nk, ng)),
        y_recv=dma((nk, ng)),
        yb_send=dma((nk, ng)),
        yb_recv=dma((nk, ng)),
        ring_send=dma((WAVES, nk, 2)),
        ring_recv=dma((WAVES, nk, HOPS)),
        back_send=dma((WAVES, nk, 2)),
        back_recv=dma((WAVES, nk, HOPS)),
        gx_send=dma((spans,)),
        gx_recv=dma((spans,)),
        gf_send=dma((spans,)),
        gf_recv=dma((spans,)),
        gm_send=dma((spans,)),
        gm_recv=dma((spans,)),
        rm_send=dma((spans,)),
        rm_recv=dma((spans,)),
        rf_send=dma((spans,)),
        rf_recv=dma((spans,)),
        rn_send=dma((spans,)),
        rn_recv=dma((spans,)),
    )
    leaves, treedef = jax.tree_util.tree_flatten(scratch)
    anywhere = pl.BlockSpec(memory_space=pl.ANY)
    results = pl.pallas_call(
        functools.partial(fused_kernel, n_dp, n_tp, treedef),
        out_shape=[
            jax.ShapeDtypeStruct(queries.shape, bf16),
            jax.ShapeDtypeStruct(queries.shape, bf16),
            jax.ShapeDtypeStruct((n_slabs, ts, enc), jnp.float32),
        ],
        in_specs=[pl.BlockSpec(memory_space=pltpu.SMEM)] * 2 + [anywhere] * 5,
        out_specs=[anywhere, anywhere, pl.BlockSpec(memory_space=pltpu.VMEM)],
        scratch_shapes=leaves,
        compiler_params=pltpu.CompilerParams(
            collective_id=0, has_side_effects=True, vmem_limit_bytes=VMEM_LIMIT
        ),
        name="spanned",
    )(owners.T, slots.T, table, queries, cotangent, key_weight, value_weight)
    return finish(*results)


def solution(mesh):
    in_specs = (
        P("dp", "tensor"),
        P("dp", "tensor"),
        P("dp", None, None),
        P(None, "tensor"),
        P(None, "tensor"),
        P("dp", None),
        P("dp", None),
    )
    out_specs = (P("dp", "tensor"), P("dp", "tensor"), P("dp", "tensor", None))
    return jax.shard_map(
        on_device, mesh=mesh, in_specs=in_specs, out_specs=out_specs, check_vma=False
    )
```
